512 devices in a mesh: row: 32 (over x, y), col: 16 (over z, core).
Axes of the slice: x: 4, y: 8, z: 8, core: 2. Of those that a mesh axis runs over, the one named last changes fastest.
Arguments:
- vectors: float32 [16384, 16384], P('row', 'col'), may hold values from -6 to 6
- reflectors_first: float32 [256, 16384], P('col', 'row'), may hold values from -0.1875 to 0.1875
- reflectors_second: float32 [256, 16384], P('col', 'row'), may hold values from -0.1875 to 0.1875
- factor_first: float32 [256, 256], replicated, as said below
- factor_second: float32 [256, 256], replicated, as said below
Outputs:
- transformed: float32 [16384, 16384], P('row', 'col')
The draws below stay inside these ranges and needn't reach their ends.
Inputs may be any that keep to these rules, and one draw needn't show every extreme that they name: `factor_first`: upper triangular: zero below the diagonal, diagonal between 1 and 2. `factor_second`: upper triangular: zero below the diagonal, diagonal between 1 and 2.
All inputs are finite; a program needn't handle non-finite values.
Results may differ from the reference program's by a relative error of at most 0.00014.
Values sent between devices are 32-bit elements; how exact they have to be, the bound alone decides.
No kernel may reach another device: no remote copies, remote signals or barrier semaphores. Data moves between devices by JAX's collectives and lax.ppermute only.
A program may use at most 64 MiB of HBM per device.

```python
import jax
import jax.numpy as jnp
from jax import lax

NB = 256
N = 16384
M = 16384


def upper_factor(key, spread):
    diag_key, off_key = jax.random.split(key)
    rows = lax.broadcasted_iota(jnp.int32, (NB, NB), 0)
    cols = lax.broadcasted_iota(jnp.int32, (NB, NB), 1)
    diagonal = jax.random.uniform(diag_key, (NB, NB), jnp.float32, 1.0, 2.0)
    above = spread * jax.random.normal(off_key, (NB, NB), jnp.float32)
    return jnp.where(rows == cols, diagonal, jnp.where(cols > rows, above, 0.0)).astype(jnp.float32)


def draw_factor_first(key, part):
    key = jax.random.fold_in(key, 11)
    return upper_factor(key, 0.1)


def draw_factor_second(key, part):
    key = jax.random.fold_in(key, 23)
    return upper_factor(key, 0.1)


def level_of(own_key, shape, pieces, smallest, largest):
    level = 1.0
    for dim, blocks in pieces:
        steps = jax.random.uniform(jax.random.fold_in(jax.random.fold_in(own_key, 6), dim), (blocks,), jnp.float32, smallest / len(pieces), largest / len(pieces))
        level = level * jnp.repeat(jnp.exp(steps), shape[dim] // blocks).reshape((-1,) + (1,) * (len(shape) - 1 - dim))
    return level


def scatter_about(own_key, dims, width, bound, cuts=(), dtype=jnp.bfloat16):
    entries = jax.random.normal(own_key, dims, jnp.float32) * width
    if len(cuts) > 0:
        entries = level_of(own_key, dims, cuts, -0.22, 0.18) * entries
    return jnp.clip(entries, min=-bound, max=bound).astype(dtype)


def setup_inputs(seed: int = 0) -> dict:
    key_list = jax.random.split(jax.random.key(seed), 6)
    return {
        "vectors": scatter_about(key_list[0], (N, M), 1.0, 6.0, ((0, 32), (1, 16)), jnp.float32),
        "reflectors_first": scatter_about(key_list[1], (NB, N), (N // 16) ** -0.5, 0.1875, ((0, 16), (1, 32)), jnp.float32),
        "reflectors_second": scatter_about(key_list[2], (NB, N), (N // 16) ** -0.5, 0.1875, ((0, 16), (1, 32)), jnp.float32),
        "factor_first": draw_factor_first(jax.random.fold_in(key_list[5], 71), 0),
        "factor_second": draw_factor_second(jax.random.fold_in(key_list[5], 71), 0),
    }


def apply_panel(block, panel, factor):
    proj = jnp.dot(panel, block, precision=lax.Precision.HIGHEST, preferred_element_type=jnp.float32)
    coeff = jnp.dot(factor, proj, precision=lax.Precision.HIGHEST, preferred_element_type=jnp.float32)
    update = lax.dot_general(panel, coeff, (((0,), (0,)), ((), ())), precision=lax.Precision.HIGHEST, preferred_element_type=jnp.float32)
    return block - update


def reference(vectors, reflectors_first, reflectors_second, factor_first, factor_second):
    middle = apply_panel(vectors, reflectors_second, factor_second)
    return apply_panel(middle, reflectors_first, factor_first)
```

```python
import jax
import jax.numpy as jnp
from jax import lax
from jax.sharding import Mesh, PartitionSpec as P

ROW = ("x", "y")
COL = ("z", "core")
SIZES = {"x": 4, "y": 8, "z": 8, "core": 2}


def dot(left, right, dims):
    return lax.dot_general(
        left, right, (dims, ((), ())), precision=lax.Precision.HIGH, preferred_element_type=jnp.float32
    )


def scatter_sum(value, axis):
    n = SIZES[axis]
    pieces = value.reshape(n, value.shape[0] // n, value.shape[1])
    return jnp.sum(lax.all_to_all(pieces, axis, 0, 0), axis=0)


def spread(value, axis):
    n = SIZES[axis]
    copies = jnp.broadcast_to(value[None], (n,) + value.shape)
    return lax.all_to_all(copies, axis, 0, 0).reshape(n * value.shape[0], value.shape[1])


def sum_over_rows(value):
    share = scatter_sum(scatter_sum(value, "x"), "y")
    return spread(spread(share, "y"), "x")


def fetch_panel(shard):
    return lax.all_gather(shard, COL, axis=0, tiled=True)


def local(vectors, reflectors_first, reflectors_second, factor_first, factor_second):
    second = fetch_panel(reflectors_second)
    proj_second = sum_over_rows(dot(second, vectors, ((1,), (0,))))
    first = fetch_panel(reflectors_first)
    proj_first = sum_over_rows(dot(first, vectors, ((1,), (0,))))
    cross_share = dot(reflectors_first, second, ((1,), (1,)))
    cross_share = jnp.sum(lax.all_gather(cross_share, ROW, axis=0, tiled=False), axis=0)
    cross = fetch_panel(cross_share)
    w_first = dot(factor_first, first, ((0,), (0,)))
    w_second = dot(factor_second, second - dot(cross, w_first, ((0,), (0,))), ((0,), (0,)))
    middle = vectors - dot(w_second, proj_second, ((0,), (0,)))
    return middle - dot(w_first, proj_first, ((0,), (0,)))


def solution(mesh):
    fine = Mesh(mesh.devices.reshape(4, 8, 8, 2), ("x", "y", "z", "core"))
    return jax.shard_map(
        local,
        mesh=fine,
        in_specs=(P(ROW, COL), P(COL, ROW), P(COL, ROW), P(), P()),
        out_specs=P(ROW, COL),
        check_vma=False,
    )
```

```python
import jax
import jax.numpy as jnp
from jax import lax
from jax.experimental import pallas as pl
from jax.experimental.pallas import tpu as pltpu
from jax.sharding import Mesh, PartitionSpec as P

ROW = ("x", "y")
COL = ("z", "core")
NX, NY, NZ = 4, 8, 8
F32, BF16 = jnp.float32, jnp.bfloat16
VMEM = pl.BlockSpec(memory_space=pltpu.VMEM)
SMEM = pl.BlockSpec(memory_space=pltpu.SMEM)
PARAMS = pltpu.CompilerParams(vmem_limit_bytes=40 * 2**20)

STRIDED = [
    [(sx + dx) * NY + sy + dy for dx in range(0, NX, 2) for dy in range(0, NY, 2)]
    for sx in range(2)
    for sy in range(2)
]


def partner(i, n, start):
    return (i + 1) % n if (i - start) % 2 == 0 else (i - 1) % n


def exchange(values, start):
    got = []
    for d in (1, 2, 3):
        pairs = []
        for x in range(NX):
            for y in range(NY):
                px = partner(x, NX, start) if d & 2 else x
                py = partner(y, NY, start) if d & 1 else y
                pairs.append((x * NY + y, px * NY + py))
        got.append(lax.ppermute(values[d - 1], ROW, pairs))
    return got


def split(value):
    high = value.astype(BF16)
    return high, (value - high.astype(F32)).astype(BF16)


def mul(a, b):
    return jnp.dot(a, b, preferred_element_type=F32)


def mul3(a, b):
    return mul(a[0], b[0]) + (mul(a[0], b[1]) + mul(a[1], b[0]))


def project_kernel(j_ref, second_ref, first_ref, own_ref, block_ref, *refs):
    outs, (high, low) = refs[:8], refs[8:]
    j = j_ref[0]
    for panel, ref in enumerate((second_ref, first_ref)):
        for d in range(4):
            h, l = split(ref[pl.ds(pl.multiple_of((j ^ d) * 64, 64), 64), :])
            at = pl.ds(panel * 256 + d * 64, 64)
            high[at, :] = h
            low[at, :] = l
    for t in range(4):
        cols = pl.ds(t * 256, 256)
        value = mul3((high[...], low[...]), split(block_ref[:, cols]))
        for s in range(8):
            outs[s][:64, cols] = value[s * 64 : (s + 1) * 64]
    own = split(own_ref[...])
    whole = split(second_ref[...])
    nt = lambda a, b: lax.dot_general(a, b, (((1,), (1,)), ((), ())), preferred_element_type=F32)
    cross = nt(own[0], whole[0]) + (nt(own[0], whole[1]) + nt(own[1], whole[0]))
    for d in range(4):
        outs[d][64:, :256] = cross[:8]
        outs[d][64:, 256:512] = cross[8:]
        outs[d][64:, 512:] = jnp.zeros((8, 512), F32)


def near_kernel(*refs):
    parts, out = refs[:8], refs[8]
    total = [
        (parts[4 * p][...] + parts[4 * p + 1][...]) + (parts[4 * p + 2][...] + parts[4 * p + 3][...]) for p in range(2)
    ]
    cross = total[0][64:]
    for m in range(8):
        out[m, :8, :1024] = total[0][m * 8 : m * 8 + 8]
        out[m, 8:, :1024] = total[1][m * 8 : m * 8 + 8]
        out[m, :8, 1024:] = cross[:, :256]
        out[m, 8:, 1024:] = cross[:, 256:512]


def far_kernel(parts, out, cross):
    total = ((parts[0] + parts[1]) + (parts[2] + parts[3])) + ((parts[4] + parts[5]) + (parts[6] + parts[7]))
    for m in range(8):
        out[m] = total[:, :1024]
    cross[...] = total[:, 1024:]


def part_kernel(shares, out_second, out_first):
    for m in range(8):
        out_second[m * 8 : m * 8 + 8] = shares[m, :8]
        out_first[m * 8 : m * 8 + 8] = shares[m, 8:]


def weight_kernel(j_ref, second_ref, first_ref, high, low, rows):
    j = j_ref[0]
    for panel, ref in enumerate((second_ref, first_ref)):
        for d in range(4):
            rows[pl.ds(panel * 256 + d * 64, 64), :] = ref[pl.ds(pl.multiple_of((j ^ d) * 64, 64), 64), :]
    h, l = split(rows[...].T)
    high[...] = h
    low[...] = l


def update_kernel(block_ref, wh_ref, wl_ref, *refs):
    parts, (out, high, low) = refs[:8], refs[8:]
    for s in range(8):
        h, l = split(parts[s][...])
        high[pl.ds(s * 64, 64), :] = h
        low[pl.ds(s * 64, 64), :] = l
    for t in range(4):
        cols = pl.ds(t * 256, 256)
        out[:, cols] = block_ref[:, cols] - mul3((wh_ref[...], wl_ref[...]), (high[:, cols], low[:, cols]))


def call(kernel, outs, args, scratch=(), scalars=0):
    single = not isinstance(outs, list)
    return pl.pallas_call(
        kernel,
        out_shape=outs,
        in_specs=[SMEM] * scalars + [VMEM] * (len(args) - scalars),
        out_specs=VMEM if single else [VMEM] * len(outs),
        scratch_shapes=list(scratch),
        compiler_params=PARAMS,
    )(*args)


def shape(*dims, dtype=F32):
    return jax.ShapeDtypeStruct(dims, dtype)


def exact(left, right, dims):
    return lax.dot_general(left, right, (dims, ((), ())), precision=lax.Precision.HIGHEST, preferred_element_type=F32)


def fetch_beside(shard, core):
    mine = lax.all_to_all(jnp.broadcast_to(shard[None], (NZ,) + shard.shape), "z", 0, 0)
    other = lax.ppermute(mine, "core", [(0, 1), (1, 0)])
    low = jnp.where(core == 0, mine, other)
    high = jnp.where(core == 0, other, mine)
    return jnp.stack([low, high], axis=1).reshape(-1, shard.shape[1])


def local(vectors, reflectors_first, reflectors_second, factor_first, factor_second):
    core = lax.axis_index("core")
    j = ((lax.axis_index("x") % 2) * 2 + lax.axis_index("y") % 2).astype(jnp.int32).reshape(1)
    second = lax.all_gather(reflectors_second, COL, axis=0, tiled=True)
    first = fetch_beside(reflectors_first, core)
    wide = pltpu.VMEM((512, 512), BF16)
    parts = call(
        project_kernel,
        [shape(72, 1024)] * 4 + [shape(64, 1024)] * 4,
        (j, second, first, reflectors_first, vectors),
        scratch=(wide, wide),
        scalars=1,
    )
    got_second = exchange(parts[1:4], 0)
    got_first = exchange(parts[5:8], 1)
    pieces = call(near_kernel, shape(8, 16, 1280), (parts[0], *got_second, parts[4], *got_first))
    pieces = lax.all_to_all(pieces, ROW, 0, 0, axis_index_groups=STRIDED)
    copies, cross = call(far_kernel, [shape(8, 16, 1024), shape(16, 256)], (pieces,))
    shares = lax.all_to_all(copies, ROW, 0, 0, axis_index_groups=STRIDED)
    cross = lax.all_gather(cross, COL, axis=0, tiled=True)
    share_second, share_first = call(part_kernel, [shape(64, 1024)] * 2, (shares,))
    got_second = exchange([share_second] * 3, 0)
    got_first = exchange([share_first] * 3, 1)
    w_first = exact(factor_first, first, ((0,), (0,)))
    w_second = exact(factor_second, second - exact(cross, w_first, ((0,), (0,))), ((0,), (0,)))
    weights = call(
        weight_kernel,
        [shape(512, 512, dtype=BF16)] * 2,
        (j, w_second, w_first),
        scratch=(pltpu.VMEM((512, 512), F32),),
        scalars=1,
    )
    tall = pltpu.VMEM((512, 1024), BF16)
    return call(
        update_kernel,
        shape(512, 1024),
        (vectors, *weights, share_second, *got_second, share_first, *got_first),
        scratch=(tall, tall),
    )


def solution(mesh):
    fine = Mesh(mesh.devices.reshape(NX, NY, NZ, 2), ROW + COL)
    return jax.shard_map(
        local,
        mesh=fine,
        in_specs=(P(ROW, COL), P(COL, ROW), P(COL, ROW), P(), P()),
        out_specs=P(ROW, COL),
        check_vma=False,
    )
```

```python
import jax
import jax.numpy as jnp
from jax import lax
from jax.experimental import pallas as pl
from jax.experimental.pallas import tpu as pltpu
from jax.sharding import Mesh, PartitionSpec as P

ROW = ("x", "y")
COL = ("z", "core")
NX, NY, NZ = 4, 8, 8
F32, BF16 = jnp.float32, jnp.bfloat16
VMEM = pl.BlockSpec(memory_space=pltpu.VMEM)
PARAMS = pltpu.CompilerParams(vmem_limit_bytes=48 * 2**20)

NEAR = [[x * NY + y + dy for x in range(NX) for dy in range(2)] for y in range(0, NY, 2)]
FAR = [[x * NY + y for y in range(parity, NY, 2)] for x in range(NX) for parity in range(2)]


def split(value):
    high = value.astype(BF16)
    return high, (value - high.astype(F32)).astype(BF16)


def mul(a, b):
    return jnp.dot(a, b, preferred_element_type=F32)


def mul_nt(a, b):
    return lax.dot_general(a, b, (((1,), (1,)), ((), ())), preferred_element_type=F32)


def mul3(a, b, mul=mul):
    return mul(a[0], b[0]) + (mul(a[0], b[1]) + mul(a[1], b[0]))


def project_kernel(second_ref, first_ref, own_ref, block_ref, out, high, low):
    for panel, ref in enumerate((second_ref, first_ref)):
        h, l = split(ref[...])
        high[pl.ds(panel * 256, 256), :] = h
        low[pl.ds(panel * 256, 256), :] = l
    for t in range(4):
        value = mul3((high[...], low[...]), split(block_ref[:, t * 256 : (t + 1) * 256]))
        for m in range(8):
            for half in range(2):
                at = (2 * t + half) * 64
                out[m, at : at + 64, :] = value[m * 64 : (m + 1) * 64, half * 128 : (half + 1) * 128]
    cross = mul3(split(own_ref[...]), (high[:256], low[:256]), mul_nt)
    for m in range(8):
        out[m, 512:528, :] = cross[:, :128]
        out[m, 528:544, :] = cross[:, 128:]


def near_kernel(parts, out):
    total = ((parts[0] + parts[1]) + (parts[2] + parts[3])) + ((parts[4] + parts[5]) + (parts[6] + parts[7]))
    for m in range(4):
        out[m, :128, :] = total[m * 128 : (m + 1) * 128]
        out[m, 128:, :] = total[512:]


def far_kernel(parts, out, cross):
    total = (parts[0] + parts[1]) + (parts[2] + parts[3])
    for m in range(4):
        out[m] = total[:128]
    cross[:, :128] = total[128:144]
    cross[:, 128:] = total[144:]


def copy_kernel(share, out):
    for m in range(8):
        out[m] = share[...]


def weight_kernel(second_ref, first_ref, high, low):
    for panel, ref in enumerate((second_ref, first_ref)):
        h, l = split(ref[...].T)
        high[:, panel * 256 : (panel + 1) * 256] = h
        low[:, panel * 256 : (panel + 1) * 256] = l


def update_kernel(block_ref, wh_ref, wl_ref, proj_ref, out):
    proj = jnp.concatenate(
        [jnp.concatenate([proj_ref[m, :64], proj_ref[m, 64:]], axis=1) for m in range(8)], axis=0
    )
    out[...] = block_ref[...] - mul3((wh_ref[...], wl_ref[...]), split(proj))


def call(kernel, outs, args, scratch=()):
    single = not isinstance(outs, list)
    return pl.pallas_call(
        kernel,
        out_shape=outs,
        in_specs=[VMEM] * len(args),
        out_specs=VMEM if single else [VMEM] * len(outs),
        scratch_shapes=list(scratch),
        compiler_params=PARAMS,
    )(*args)


def shape(*dims, dtype=F32):
    return jax.ShapeDtypeStruct(dims, dtype)


def exact(left, right):
    dims = (((0,), (0,)), ((), ()))
    return lax.dot_general(left, right, dims, precision=lax.Precision.HIGHEST, preferred_element_type=F32)


def trade(pieces, groups):
    return lax.all_to_all(pieces, ROW, 0, 0, axis_index_groups=groups)


def local(vectors, reflectors_first, reflectors_second, factor_first, factor_second):
    copies = jnp.broadcast_to(reflectors_first[None], (2 * NZ,) + reflectors_first.shape)
    first = lax.all_to_all(copies, COL, 0, 0).reshape(256, 512)
    second = lax.all_gather(reflectors_second, COL, axis=0, tiled=True)
    wide = pltpu.VMEM((512, 512), BF16)
    parts = call(project_kernel, shape(8, 544, 128), (second, first, reflectors_first, vectors), (wide, wide))
    parts = call(near_kernel, shape(4, 160, 128), (trade(parts, NEAR),))
    share, cross = call(far_kernel, [shape(4, 128, 128), shape(16, 256)], (trade(parts, FAR),))
    share = trade(share, FAR).reshape(512, 128)
    proj = trade(call(copy_kernel, shape(8, 512, 128), (share,)), NEAR)
    cross = lax.all_gather(cross, COL, axis=0, tiled=True)
    w_first = exact(factor_first, first)
    w_second = exact(factor_second, second - exact(cross, w_first))
    weights = call(weight_kernel, [shape(512, 512, dtype=BF16)] * 2, (w_second, w_first))
    return pl.pallas_call(
        update_kernel,
        out_shape=shape(512, 1024),
        grid=(4,),
        in_specs=[
            pl.BlockSpec((512, 256), lambda t: (0, t)),
            pl.BlockSpec((512, 512), lambda t: (0, 0)),
            pl.BlockSpec((512, 512), lambda t: (0, 0)),
            pl.BlockSpec((8, 128, 128), lambda t: (0, t, 0)),
        ],
        out_specs=pl.BlockSpec((512, 256), lambda t: (0, t)),
        compiler_params=PARAMS,
    )(vectors, *weights, proj)


def solution(mesh):
    fine = Mesh(mesh.devices.reshape(NX, NY, NZ, 2), ROW + COL)
    return jax.shard_map(
        local,
        mesh=fine,
        in_specs=(P(ROW, COL), P(COL, ROW), P(COL, ROW), P(), P()),
        out_specs=P(ROW, COL),
        check_vma=False,
    )
```

```python
import jax
import jax.numpy as jnp
from jax import lax
from jax.experimental import pallas as pl
from jax.experimental.pallas import tpu as pltpu
from jax.sharding import Mesh, PartitionSpec as P

ROW = ("x", "y")
COL = ("z", "core")
NX, NY, NZ = 4, 8, 8
F32, BF16 = jnp.float32, jnp.bfloat16
VMEM = pl.BlockSpec(memory_space=pltpu.VMEM)
PARAMS = pltpu.CompilerParams(vmem_limit_bytes=24 * 2**20)

NEAR = [[x * NY + y + dy for x in range(NX) for dy in range(2)] for y in range(0, NY, 2)]
FAR = [[x * NY + y for y in range(parity, NY, 2)] for x in range(NX) for parity in range(2)]


def split(value):
    high = value.astype(BF16)
    return high, (value - high.astype(F32)).astype(BF16)


def mul(a, b):
    return jnp.dot(a, b, preferred_element_type=F32)


def mul_nt(a, b):
    return lax.dot_general(a, b, (((1,), (1,)), ((), ())), preferred_element_type=F32)


def mul3(a, b, mul=mul):
    return mul(a[0], b[0]) + (mul(a[0], b[1]) + mul(a[1], b[0]))


def project(panel, block_ref, out):
    for t in range(4):
        value = mul3(panel, split(block_ref[:, t * 256 : (t + 1) * 256]))
        for m in range(8):
            for half in range(2):
                at = (2 * t + half) * 32
                out[m, at : at + 32, :] = value[m * 32 : (m + 1) * 32, half * 128 : (half + 1) * 128]


def second_kernel(second_ref, own_ref, block_ref, out):
    panel = split(second_ref[...])
    project(panel, block_ref, out)
    cross = mul3(split(own_ref[...]), panel, mul_nt)
    for m in range(8):
        out[m, 256:272, :] = cross[:, :128]
        out[m, 272:288, :] = cross[:, 128:]


def first_kernel(first_ref, block_ref, out):
    project(split(first_ref[...]), block_ref, out)


def sum8(parts):
    return ((parts[0] + parts[1]) + (parts[2] + parts[3])) + ((parts[4] + parts[5]) + (parts[6] + parts[7]))


def near_kernel(second_parts, first_parts, out):
    second, first = sum8(second_parts), sum8(first_parts)
    for m in range(4):
        out[m, :64, :] = second[m * 64 : (m + 1) * 64]
        out[m, 64:128, :] = first[m * 64 : (m + 1) * 64]
        out[m, 128:, :] = second[256:]


def far_kernel(parts, out, cross):
    total = (parts[0] + parts[1]) + (parts[2] + parts[3])
    for m in range(4):
        out[m] = total[:128]
    cross[:, :128] = total[128:144]
    cross[:, 128:] = total[144:]


def copy_kernel(share, out):
    for m in range(8):
        for n in range(4):
            out[m, n * 64 : (n + 1) * 64, :] = share[n, :64]
            out[m, 256 + n * 64 : 256 + (n + 1) * 64, :] = share[n, 64:]


def weight_kernel(second_ref, first_ref, high, low):
    for panel, ref in enumerate((second_ref, first_ref)):
        h, l = split(ref[...].T)
        high[:, panel * 256 : (panel + 1) * 256] = h
        low[:, panel * 256 : (panel + 1) * 256] = l


def update_kernel(block_ref, wh_ref, wl_ref, second_ref, first_ref, out):
    rows = [jnp.concatenate([ref[m, :32], ref[m, 32:]], axis=1) for ref in (second_ref, first_ref) for m in range(8)]
    proj = split(jnp.concatenate(rows, axis=0))
    out[...] = block_ref[...] - mul3((wh_ref[...], wl_ref[...]), proj)


def call(kernel, outs, args, scratch=()):
    single = not isinstance(outs, list)
    return pl.pallas_call(
        kernel,
        out_shape=outs,
        in_specs=[VMEM] * len(args),
        out_specs=VMEM if single else [VMEM] * len(outs),
        scratch_shapes=list(scratch),
        compiler_params=PARAMS,
    )(*args)


def shape(*dims, dtype=F32):
    return jax.ShapeDtypeStruct(dims, dtype)


def exact(left, right):
    dims = (((0,), (0,)), ((), ()))
    return lax.dot_general(left, right, dims, precision=lax.Precision.HIGHEST, preferred_element_type=F32)


def trade(pieces, groups):
    return lax.all_to_all(pieces, ROW, 0, 0, axis_index_groups=groups)


def local(vectors, reflectors_first, reflectors_second, factor_first, factor_second):
    second = lax.all_gather(reflectors_second, COL, axis=0, tiled=True)
    second_parts = call(second_kernel, shape(8, 288, 128), (second, reflectors_first, vectors))
    second_parts = trade(second_parts, NEAR)
    first = lax.all_gather(reflectors_first, COL, axis=0, tiled=True)
    first_parts = trade(call(first_kernel, shape(8, 256, 128), (first, vectors)), NEAR)
    parts = call(near_kernel, shape(4, 160, 128), (second_parts, first_parts))
    share, cross = call(far_kernel, [shape(4, 128, 128), shape(16, 256)], (trade(parts, FAR),))
    proj = trade(call(copy_kernel, shape(8, 512, 128), (trade(share, FAR),)), NEAR)
    cross = lax.all_gather(cross, COL, axis=0, tiled=True)
    w_first = exact(factor_first, first)
    w_second = exact(factor_second, second - exact(cross, w_first))
    weights = call(weight_kernel, [shape(512, 512, dtype=BF16)] * 2, (w_second, w_first))
    return pl.pallas_call(
        update_kernel,
        out_shape=shape(512, 1024),
        grid=(4,),
        in_specs=[
            pl.BlockSpec((512, 256), lambda t: (0, t)),
            pl.BlockSpec((512, 512), lambda t: (0, 0)),
            pl.BlockSpec((512, 512), lambda t: (0, 0)),
            pl.BlockSpec((8, 64, 128), lambda t: (0, t, 0)),
            pl.BlockSpec((8, 64, 128), lambda t: (0, t + 4, 0)),
        ],
        out_specs=pl.BlockSpec((512, 256), lambda t: (0, t)),
        compiler_params=PARAMS,
    )(vectors, *weights, proj, proj)


def solution(mesh):
    fine = Mesh(mesh.devices.reshape(NX, NY, NZ, 2), ROW + COL)
    return jax.shard_map(
        local,
        mesh=fine,
        in_specs=(P(ROW, COL), P(COL, ROW), P(COL, ROW), P(), P()),
        out_specs=P(ROW, COL),
        check_vma=False,
    )
```

```python
import jax
import jax.numpy as jnp
from jax import lax
from jax.experimental import pallas as pl
from jax.experimental.pallas import tpu as pltpu
from jax.sharding import Mesh, PartitionSpec as P

ROW = ("x", "y")
COL = ("z", "core")
NX, NY, NZ = 4, 8, 8
F32, BF16 = jnp.float32, jnp.bfloat16
VMEM = pl.BlockSpec(memory_space=pltpu.VMEM)
SMEM = pl.BlockSpec(memory_space=pltpu.SMEM)
HBM = pl.BlockSpec(memory_space=pltpu.HBM)
PARAMS = pltpu.CompilerParams(vmem_limit_bytes=48 * 2**20)

NEAR = [[x * NY + y + dy for x in range(NX) for dy in range(2)] for y in range(0, NY, 2)]
FAR = [[x * NY + y for y in range(parity, NY, 2)] for x in range(NX) for parity in range(2)]


def split(value):
    high = value.astype(BF16)
    return high, (value - high.astype(F32)).astype(BF16)


def mul(a, b):
    return jnp.dot(a, b, preferred_element_type=F32)


def mul_nt(a, b):
    return lax.dot_general(a, b, (((1,), (1,)), ((), ())), preferred_element_type=F32)


def mul3(a, b, mul=mul):
    return mul(a[0], b[0]) + (mul(a[0], b[1]) + mul(a[1], b[0]))


def split_kernel(block_ref, high, low):
    high[...], low[...] = split(block_ref[...])


def project_kernel(core_ref, mine_ref, other_ref, own_ref, block_high, block_low, out, high, low, both):
    core = core_ref[0]
    both[0] = mine_ref[...]
    both[1] = other_ref[...]
    for c in range(2):
        from_core = both.at[core ^ c]
        for z in range(8):
            for panel in range(2):
                h, l = split(from_core[z, panel * 16 : panel * 16 + 16, :])
                at = panel * 256 + z * 32 + c * 16
                high[at : at + 16, :] = h
                low[at : at + 16, :] = l
    for t in range(4):
        at = slice(t * 256, (t + 1) * 256)
        value = mul3((high[...], low[...]), (block_high[:, at], block_low[:, at]))
        for m in range(8):
            for half in range(2):
                at = (2 * t + half) * 64
                out[m, at : at + 64, :] = value[m * 64 : (m + 1) * 64, half * 128 : (half + 1) * 128]
    cross = mul3(split(own_ref[...]), (high[:256], low[:256]), mul_nt)
    for m in range(8):
        out[m, 512:528, :] = cross[:, :128]
        out[m, 528:544, :] = cross[:, 128:]


def near_kernel(parts, out):
    total = ((parts[0] + parts[1]) + (parts[2] + parts[3])) + ((parts[4] + parts[5]) + (parts[6] + parts[7]))
    for m in range(4):
        out[m, :128, :] = total[m * 128 : (m + 1) * 128]
        out[m, 128:, :] = total[512:]


def far_kernel(parts, out, cross):
    total = (parts[0] + parts[1]) + (parts[2] + parts[3])
    for m in range(4):
        out[m] = total[:128]
    cross[:, :128] = total[128:144]
    cross[:, 128:] = total[144:]


def copy_kernel(share, out, sems):
    copies = [pltpu.make_async_copy(share, out.at[m], sems.at[m]) for m in range(8)]
    for copy in copies:
        copy.start()
    for copy in copies:
        copy.wait()


def weight_kernel(second_ref, first_ref, out):
    for panel, ref in enumerate((second_ref, first_ref)):
        out[0, :, panel * 256 : (panel + 1) * 256], out[1, :, panel * 256 : (panel + 1) * 256] = split(ref[...].T)


def update_kernel(block_ref, w_ref, proj_ref, out_ref, block, parts, out, block_sems, part_sems, out_sems):
    at = [slice(t * 256, (t + 1) * 256) for t in range(4)]
    rows = [slice(t * 128, (t + 1) * 128) for t in range(4)]
    reads = [pltpu.make_async_copy(proj_ref.at[:, rows[t]], parts.at[:, rows[t]], part_sems.at[t]) for t in range(4)]
    reads += [pltpu.make_async_copy(block_ref.at[:, at[t]], block.at[:, at[t]], block_sems.at[t]) for t in range(4)]
    writes = [pltpu.make_async_copy(out.at[:, at[t]], out_ref.at[:, at[t]], out_sems.at[t]) for t in range(4)]
    for read in reads:
        read.start()
    for t in range(4):
        first = t * 128
        reads[t].wait()
        proj = jnp.concatenate(
            [
                jnp.concatenate([parts[m, first : first + 64], parts[m, first + 64 : first + 128]], axis=1)
                for m in range(8)
            ],
            axis=0,
        )
        change = mul3((w_ref[0], w_ref[1]), split(proj))
        reads[4 + t].wait()
        out[:, at[t]] = block[:, at[t]] - change
        writes[t].start()
    for write in writes:
        write.wait()


def call(kernel, outs, args, scratch=(), scalars=0, inputs=None, out_spec=VMEM):
    single = not isinstance(outs, list)
    return pl.pallas_call(
        kernel,
        out_shape=outs,
        in_specs=inputs or [SMEM] * scalars + [VMEM] * (len(args) - scalars),
        out_specs=out_spec if single else [out_spec] * len(outs),
        scratch_shapes=list(scratch),
        compiler_params=PARAMS,
    )(*args)


def shape(*dims, dtype=F32):
    return jax.ShapeDtypeStruct(dims, dtype)


def exact(left, right):
    dims = (((0,), (0,)), ((), ()))
    return lax.dot_general(left, right, dims, precision=lax.Precision.HIGHEST, preferred_element_type=F32)


def trade(pieces, groups):
    return lax.all_to_all(pieces, ROW, 0, 0, axis_index_groups=groups)


def local(vectors, reflectors_first, reflectors_second, factor_first, factor_second):
    core = lax.axis_index("core")
    shards = jnp.concatenate([reflectors_second, reflectors_first], axis=0)
    mine = lax.all_to_all(jnp.broadcast_to(shards[None], (NZ,) + shards.shape), "z", 0, 0)
    other = lax.ppermute(mine, "core", [(0, 1), (1, 0)])
    wide = pltpu.VMEM((512, 512), BF16)
    block = call(split_kernel, [shape(512, 1024, dtype=BF16)] * 2, (vectors,))
    parts = call(
        project_kernel,
        shape(8, 544, 128),
        (core.astype(jnp.int32).reshape(1), mine, other, reflectors_first, *block),
        (wide, wide, pltpu.VMEM((2, 8, 32, 512), F32)),
        scalars=1,
    )
    parts = call(near_kernel, shape(4, 160, 128), (trade(parts, NEAR),))
    share, cross = call(far_kernel, [shape(4, 128, 128), shape(16, 256)], (trade(parts, FAR),))
    share = trade(share, FAR).reshape(512, 128)
    copies = call(copy_kernel, shape(8, 512, 128), (share,), (pltpu.SemaphoreType.DMA((8,)),), out_spec=HBM)
    proj = trade(copies, NEAR)
    cross = lax.all_gather(cross, COL, axis=0, tiled=True)
    by_core = jnp.stack([jnp.where(core == 0, mine, other), jnp.where(core == 0, other, mine)], axis=1)
    second = by_core[:, :, :16].reshape(256, 512)
    first = by_core[:, :, 16:].reshape(256, 512)
    w_first = exact(factor_first, first)
    w_second = exact(factor_second, second - exact(cross, w_first))
    weights = call(weight_kernel, shape(2, 512, 512, dtype=BF16), (w_second, w_first))
    whole = pltpu.VMEM((512, 1024), F32)
    four = pltpu.SemaphoreType.DMA((4,))
    return call(
        update_kernel,
        shape(512, 1024),
        (vectors, weights, proj),
        (whole, pltpu.VMEM((8, 512, 128), F32), whole, four, four, four),
        inputs=[HBM, VMEM, HBM],
        out_spec=HBM,
    )


def solution(mesh):
    fine = Mesh(mesh.devices.reshape(NX, NY, NZ, 2), ROW + COL)
    return jax.shard_map(
        local,
        mesh=fine,
        in_specs=(P(ROW, COL), P(COL, ROW), P(COL, ROW), P(), P()),
        out_specs=P(ROW, COL),
        check_vma=False,
    )
```

```python
import jax
import jax.numpy as jnp
from jax import lax
from jax.experimental import pallas as pl
from jax.experimental.pallas import tpu as pltpu
from jax.sharding import Mesh, PartitionSpec as P

ROW = ("x", "y")
COL = ("z", "core")
NX, NY, NZ = 4, 8, 8
F32, BF16 = jnp.float32, jnp.bfloat16
VMEM = pl.BlockSpec(memory_space=pltpu.VMEM)
SMEM = pl.BlockSpec(memory_space=pltpu.SMEM)
HBM = pl.BlockSpec(memory_space=pltpu.HBM)

NEAR = [[x * NY + y + dy for x in range(NX) for dy in range(2)] for y in range(0, NY, 2)]


def split(value):
    high = value.astype(BF16)
    return high, (value - high.astype(F32)).astype(BF16)


def mul(a, b):
    return jnp.dot(a, b, preferred_element_type=F32)


def mul_nt(a, b):
    return lax.dot_general(a, b, (((1,), (1,)), ((), ())), preferred_element_type=F32)


def mul3(a, b, mul=mul):
    return mul(a[0], b[0]) + (mul(a[0], b[1]) + mul(a[1], b[0]))


def split_kernel(block_ref, high, low):
    high[...], low[...] = split(block_ref[...])


def project(chain, block_high, block_low, out):
    for t in range(4):
        at = slice(t * 256, (t + 1) * 256)
        value = mul3(chain, (block_high[:, at], block_low[:, at]))
        for m in range(8):
            for half in range(2):
                to = (2 * t + half) * 32
                out[m, to : to + 32, :] = value[m * 32 : (m + 1) * 32, half * 128 : (half + 1) * 128]


def mine_kernel(mine_ref, block_high, block_low, out):
    project(split(mine_ref[...]), block_high, block_low, out)


def other_kernel(core_ref, mine_ref, other_ref, own_ref, block_high, block_low, out, both, second):
    project(split(other_ref[...]), block_high, block_low, out)
    core = core_ref[0]
    both[0] = mine_ref[...]
    both[1] = other_ref[...]
    for c in range(2):
        from_core = both.at[core ^ c]
        for z in range(8):
            second[z * 32 + c * 16 : z * 32 + c * 16 + 16, :] = from_core[z * 32 : z * 32 + 16, :]
    cross = mul3(split(own_ref[...]), split(second[...]), mul_nt)
    for m in range(8):
        out[m, 256:272, :] = cross[:, :128]
        out[m, 272:288, :] = cross[:, 128:]


def near_kernel(parts, out):
    out[...] = ((parts[0] + parts[1]) + (parts[2] + parts[3])) + ((parts[4] + parts[5]) + (parts[6] + parts[7]))


def add_kernel(share, got, out):
    out[...] = share[...] + got[...]


def mine_copy_kernel(share, got, out):
    total = share[...] + got[...]
    for m in range(8):
        out[m] = total


def other_copy_kernel(share, got, out, cross):
    total = share[...] + got[...]
    for m in range(8):
        out[m] = total[:256]
    cross[:, :128] = total[256:272]
    cross[:, 128:] = total[272:]


def natural(parts):
    return jnp.concatenate(
        [jnp.concatenate([parts[m, t * 32 : (t + 1) * 32] for t in range(8)], axis=1) for m in range(8)], axis=0
    )


def prepare_kernel(core_ref, second_ref, first_ref, parts, out, rows):
    core = core_ref[0]
    for c in range(2):
        for z in range(8):
            at = pl.ds(pl.multiple_of(z * 32 + (core ^ c) * 16, 16), 16)
            to = c * 256 + z * 32
            rows[to : to + 16, :] = second_ref[at, :]
            rows[to + 16 : to + 32, :] = first_ref[at, :]
    out[0], out[1] = split(rows[...].T)
    high, low = split(natural(parts))
    for half in range(2):
        out[2, half * 256 : (half + 1) * 256] = high[:, half * 512 : (half + 1) * 512]
        out[3, half * 256 : (half + 1) * 256] = low[:, half * 512 : (half + 1) * 512]


def update_kernel(block_ref, ready_ref, parts_ref, out_ref, block, ready, parts, high, low, out, reads, writes):
    loads = [pltpu.make_async_copy(parts_ref, parts, reads.at[0])]
    loads.append(pltpu.make_async_copy(ready_ref, ready, reads.at[1]))
    for t in range(2):
        rows = slice(t * 256, (t + 1) * 256)
        loads.append(pltpu.make_async_copy(block_ref.at[rows], block.at[rows], reads.at[2 + t]))
    for load in loads:
        load.start()
    loads[0].wait()
    high[256:], low[256:] = split(natural(parts))
    loads[1].wait()
    for half in range(2):
        at = slice(half * 512, (half + 1) * 512)
        high[:256, at] = ready[2, half * 256 : (half + 1) * 256]
        low[:256, at] = ready[3, half * 256 : (half + 1) * 256]
    stores = []
    for t in range(2):
        rows = slice(t * 256, (t + 1) * 256)
        loads[2 + t].wait()
        for u in range(4):
            at = slice(u * 256, (u + 1) * 256)
            change = mul3((ready[0, rows], ready[1, rows]), (high[:, at], low[:, at]))
            out[rows, at] = block[rows, at] - change
        stores.append(pltpu.make_async_copy(out.at[rows], out_ref.at[rows], writes.at[t]))
        stores[t].start()
    for store in stores:
        store.wait()


def call(kernel, outs, args, scratch=(), scalars=0, inputs=None, out_spec=VMEM, limit=48):
    single = not isinstance(outs, list)
    return pl.pallas_call(
        kernel,
        out_shape=outs,
        in_specs=inputs or [SMEM] * scalars + [VMEM] * (len(args) - scalars),
        out_specs=out_spec if single else [out_spec] * len(outs),
        scratch_shapes=list(scratch),
        compiler_params=pltpu.CompilerParams(vmem_limit_bytes=limit * 2**20),
    )(*args)


def shape(*dims, dtype=F32):
    return jax.ShapeDtypeStruct(dims, dtype)


def exact(left, right):
    dims = (((0,), (0,)), ((), ()))
    return lax.dot_general(left, right, dims, precision=lax.Precision.HIGHEST, preferred_element_type=F32)


def trade(pieces):
    return lax.all_to_all(pieces, ROW, 0, 0, axis_index_groups=NEAR)


def across(value, distance):
    return lax.ppermute(value, "y", [(y, y ^ distance) for y in range(NY)])


def local(vectors, reflectors_first, reflectors_second, factor_first, factor_second):
    core = lax.axis_index("core")
    scalar = core.astype(jnp.int32).reshape(1)
    shards = jnp.concatenate([reflectors_second, reflectors_first], axis=0)
    mine = lax.all_to_all(jnp.broadcast_to(shards[None], (NZ,) + shards.shape), "z", 0, 0).reshape(256, 512)
    other = lax.ppermute(mine, "core", [(0, 1), (1, 0)])
    block = call(split_kernel, [shape(512, 1024, dtype=BF16)] * 2, (vectors,))
    mine_parts = trade(call(mine_kernel, shape(8, 256, 128), (mine, *block)))
    panel = pltpu.VMEM((256, 512), F32)
    other_parts = trade(
        call(
            other_kernel,
            shape(8, 288, 128),
            (scalar, mine, other, reflectors_first, *block),
            (pltpu.VMEM((2, 256, 512), F32), panel),
            scalars=1,
        )
    )
    share = call(near_kernel, shape(256, 128), (mine_parts,))
    share = call(add_kernel, shape(256, 128), (share, across(share, 2)))
    mine_proj = trade(call(mine_copy_kernel, shape(8, 256, 128), (share, across(share, 4))))
    share = call(near_kernel, shape(288, 128), (other_parts,))
    share = call(add_kernel, shape(288, 128), (share, across(share, 2)))
    copies, cross = call(other_copy_kernel, [shape(8, 256, 128), shape(16, 256)], (share, across(share, 4)))
    other_proj = trade(copies)
    cross = lax.all_gather(cross, COL, axis=0, tiled=True)
    both = jnp.stack([jnp.where(core == 0, mine, other), jnp.where(core == 0, other, mine)]).reshape(2, 8, 32, 512)
    by_core = both.transpose(1, 0, 2, 3)
    second = by_core[:, :, :16].reshape(256, 512)
    first = by_core[:, :, 16:].reshape(256, 512)
    w_first = exact(factor_first, first)
    w_second = exact(factor_second, second - exact(cross, w_first))
    ready = call(
        prepare_kernel,
        shape(4, 512, 512, dtype=BF16),
        (scalar, w_second, w_first, mine_proj),
        (pltpu.VMEM((512, 512), F32),),
        scalars=1,
    )
    whole = pltpu.VMEM((512, 1024), F32)
    tall = pltpu.VMEM((512, 1024), BF16)
    return call(
        update_kernel,
        shape(512, 1024),
        (vectors, ready, other_proj),
        (
            whole,
            pltpu.VMEM((4, 512, 512), BF16),
            pltpu.VMEM((8, 256, 128), F32),
            tall,
            tall,
            whole,
            pltpu.SemaphoreType.DMA((4,)),
            pltpu.SemaphoreType.DMA((2,)),
        ),
        inputs=[HBM] * 3,
        out_spec=HBM,
        limit=58,
    )


def solution(mesh):
    fine = Mesh(mesh.devices.reshape(NX, NY, NZ, 2), ROW + COL)
    return jax.shard_map(
        local,
        mesh=fine,
        in_specs=(P(ROW, COL), P(COL, ROW), P(COL, ROW), P(), P()),
        out_specs=P(ROW, COL),
        check_vma=False,
    )
```

```python
import jax
import jax.numpy as jnp
from jax import lax
from jax.experimental import pallas as pl
from jax.experimental.pallas import tpu as pltpu
from jax.sharding import Mesh, PartitionSpec as P

ROW = ("x", "y")
COL = ("z", "core")
NX, NY, NZ = 4, 8, 8
F32, BF16 = jnp.float32, jnp.bfloat16
VMEM = pl.BlockSpec(memory_space=pltpu.VMEM)
SMEM = pl.BlockSpec(memory_space=pltpu.SMEM)
HBM = pl.BlockSpec(memory_space=pltpu.HBM)
PARAMS = pltpu.CompilerParams(vmem_limit_bytes=48 * 2**20)


def device(x, y, z, core):
    return ((x % NX * NY + y % NY) * NZ + z) * 2 + core


NEAR = [
    [device(bx + (px ^ core) + core, by + (py ^ core) + core, z, core) for px in range(2) for py in range(2)]
    for z in range(NZ)
    for core in range(2)
    for bx in range(0, NX, 2)
    for by in range(0, NY, 2)
]
FAR = [
    [device(px + dx, py + dy, z, core) for dx in range(0, NX, 2) for dy in range(0, NY, 2)]
    for z in range(NZ)
    for core in range(2)
    for px in range(2)
    for py in range(2)
]


def split(value):
    high = value.astype(BF16)
    return high, (value - high.astype(F32)).astype(BF16)


def mul(a, b):
    return jnp.dot(a, b, preferred_element_type=F32)


def mul_nt(a, b):
    return lax.dot_general(a, b, (((1,), (1,)), ((), ())), preferred_element_type=F32)


def mul3(a, b, mul=mul):
    return mul(a[0], b[0]) + (mul(a[0], b[1]) + mul(a[1], b[0]))


def split_kernel(block_ref, high, low):
    high[...], low[...] = split(block_ref[...])


def project_kernel(core_ref, mine_ref, other_ref, own_ref, block_high, block_low, out, high, low, both):
    core = core_ref[0]
    both[0] = mine_ref[...]
    both[1] = other_ref[...]
    for c in range(2):
        from_core = both.at[core ^ c]
        for z in range(8):
            for panel in range(2):
                h, l = split(from_core[z, panel * 16 : panel * 16 + 16, :])
                at = panel * 256 + z * 32 + c * 16
                high[at : at + 16, :] = h
                low[at : at + 16, :] = l
    for t in range(4):
        at = slice(t * 256, (t + 1) * 256)
        value = mul3((high[...], low[...]), (block_high[:, at], block_low[:, at]))
        for m in range(4):
            for half in range(2):
                to = (2 * t + half) * 128
                out[m, to : to + 128, :] = value[m * 128 : (m + 1) * 128, half * 128 : (half + 1) * 128]
    cross = mul3(split(own_ref[...]), (high[:256], low[:256]), mul_nt)
    for m in range(4):
        out[m, 1024:1040, :] = cross[:, :128]
        out[m, 1040:, :] = cross[:, 128:]


def near_kernel(parts, out):
    total = (parts[0] + parts[1]) + (parts[2] + parts[3])
    for m in range(8):
        out[m, :128, :] = total[m * 128 : (m + 1) * 128]
        out[m, 128:, :] = total[1024:]


def far_kernel(parts, out, cross):
    total = ((parts[0] + parts[1]) + (parts[2] + parts[3])) + ((parts[4] + parts[5]) + (parts[6] + parts[7]))
    for m in range(8):
        out[m] = total[:128]
    cross[:, :128] = total[128:144]
    cross[:, 128:] = total[144:]


def copy_kernel(share, after, out, sems):
    copies = [pltpu.make_async_copy(share, out.at[m], sems.at[m]) for m in range(4)]
    for copy in copies:
        copy.start()
    for copy in copies:
        copy.wait()


def weight_kernel(second_ref, first_ref, out):
    for panel, ref in enumerate((second_ref, first_ref)):
        out[0, :, panel * 256 : (panel + 1) * 256], out[1, :, panel * 256 : (panel + 1) * 256] = split(ref[...].T)


def update_kernel(block_ref, w_ref, parts, out_ref, block, out, reads, writes):
    rows = [slice(t * 256, (t + 1) * 256) for t in range(2)]
    loads = [pltpu.make_async_copy(block_ref.at[rows[t]], block.at[rows[t]], reads.at[t]) for t in range(2)]
    stores = [pltpu.make_async_copy(out.at[rows[t]], out_ref.at[rows[t]], writes.at[t]) for t in range(2)]
    for load in loads:
        load.start()
    whole = [jnp.concatenate([parts[m, j * 128 : (j + 1) * 128] for j in range(8)], axis=1) for m in range(4)]
    proj = split(jnp.concatenate(whole, axis=0))
    for t in range(2):
        change = mul3((w_ref[0, rows[t]], w_ref[1, rows[t]]), proj)
        loads[t].wait()
        out[rows[t]] = block[rows[t]] - change
        stores[t].start()
    for store in stores:
        store.wait()


def call(kernel, outs, args, scratch=(), scalars=0, inputs=None, out_spec=VMEM):
    single = not isinstance(outs, list)
    return pl.pallas_call(
        kernel,
        out_shape=outs,
        in_specs=inputs or [SMEM] * scalars + [VMEM] * (len(args) - scalars),
        out_specs=out_spec if single else [out_spec] * len(outs),
        scratch_shapes=list(scratch),
        compiler_params=PARAMS,
    )(*args)


def shape(*dims, dtype=F32):
    return jax.ShapeDtypeStruct(dims, dtype)


def exact(left, right):
    dims = (((0,), (0,)), ((), ()))
    return lax.dot_general(left, right, dims, precision=lax.Precision.HIGHEST, preferred_element_type=F32)


def trade(pieces, groups):
    return lax.all_to_all(pieces, ROW + COL, 0, 0, axis_index_groups=groups)


def local(vectors, reflectors_first, reflectors_second, factor_first, factor_second):
    core = lax.axis_index("core")
    shards = jnp.concatenate([reflectors_second, reflectors_first], axis=0)
    mine = lax.all_to_all(jnp.broadcast_to(shards[None], (NZ,) + shards.shape), "z", 0, 0)
    other = lax.ppermute(mine, "core", [(0, 1), (1, 0)])
    wide = pltpu.VMEM((512, 512), BF16)
    block = call(split_kernel, [shape(512, 1024, dtype=BF16)] * 2, (vectors,))
    parts = call(
        project_kernel,
        shape(4, 1056, 128),
        (core.astype(jnp.int32).reshape(1), mine, other, reflectors_first, *block),
        (wide, wide, pltpu.VMEM((2, 8, 32, 512), F32)),
        scalars=1,
    )
    parts = call(near_kernel, shape(8, 160, 128), (trade(parts, NEAR),))
    share, cross = call(far_kernel, [shape(8, 128, 128), shape(16, 256)], (trade(parts, FAR),))
    share = trade(share, FAR).reshape(1024, 128)
    cross = lax.all_gather(cross, COL, axis=0, tiled=True)
    copies = call(
        copy_kernel,
        shape(4, 1024, 128),
        (share, cross),
        (pltpu.SemaphoreType.DMA((4,)),),
        inputs=[VMEM, HBM],
        out_spec=HBM,
    )
    proj = trade(copies, NEAR)
    by_core = jnp.stack([jnp.where(core == 0, mine, other), jnp.where(core == 0, other, mine)], axis=1)
    second = by_core[:, :, :16].reshape(256, 512)
    first = by_core[:, :, 16:].reshape(256, 512)
    w_first = exact(factor_first, first)
    w_second = exact(factor_second, second - exact(cross, w_first))
    weights = call(weight_kernel, shape(2, 512, 512, dtype=BF16), (w_second, w_first))
    whole = pltpu.VMEM((512, 1024), F32)
    two = pltpu.SemaphoreType.DMA((2,))
    return call(
        update_kernel,
        shape(512, 1024),
        (vectors, weights, proj),
        (whole, whole, two, two),
        inputs=[HBM, VMEM, VMEM],
        out_spec=HBM,
    )


def solution(mesh):
    fine = Mesh(mesh.devices.reshape(NX, NY, NZ, 2), ROW + COL)
    return jax.shard_map(
        local,
        mesh=fine,
        in_specs=(P(ROW, COL), P(COL, ROW), P(COL, ROW), P(), P()),
        out_specs=P(ROW, COL),
        check_vma=False,
    )
```

```python
import jax
import jax.numpy as jnp
from jax import lax
from jax.experimental import pallas as pl
from jax.experimental.pallas import tpu as pltpu
from jax.sharding import Mesh, PartitionSpec as P

ROW = ("x", "y")
COL = ("z", "core")
NX, NY, NZ = 4, 8, 8
F32, BF16 = jnp.float32, jnp.bfloat16
VMEM = pl.BlockSpec(memory_space=pltpu.VMEM)
SMEM = pl.BlockSpec(memory_space=pltpu.SMEM)
HBM = pl.BlockSpec(memory_space=pltpu.HBM)


def device(x, y, z, core):
    return ((x * NY + y % NY) * NZ + z) * 2 + core


NEAR = [
    [device(x, y + (parity ^ core) + core, z, core) for x in range(NX) for parity in range(2)]
    for z in range(NZ)
    for core in range(2)
    for y in range(0, NY, 2)
]
FAR = [
    [device(x, y, z, core) for y in range(parity, NY, 2)]
    for z in range(NZ)
    for core in range(2)
    for x in range(NX)
    for parity in range(2)
]


def split(value):
    high = value.astype(BF16)
    return high, (value - high.astype(F32)).astype(BF16)


def mul(a, b):
    return jnp.dot(a, b, preferred_element_type=F32)


def mul_nt(a, b):
    return lax.dot_general(a, b, (((1,), (1,)), ((), ())), preferred_element_type=F32)


def mul3(a, b, mul=mul):
    return mul(a[0], b[0]) + (mul(a[0], b[1]) + mul(a[1], b[0]))


def split_kernel(block_ref, high, low):
    high[...], low[...] = split(block_ref[...])


def project_kernel(core_ref, mine_ref, other_ref, own_ref, block_high, block_low, out, high, low, both):
    core = core_ref[0]
    both[0] = mine_ref[...]
    both[1] = other_ref[...]
    for c in range(2):
        from_core = both.at[core ^ c]
        for z in range(8):
            for panel in range(2):
                h, l = split(from_core[z, panel * 16 : panel * 16 + 16, :])
                at = panel * 256 + z * 32 + c * 16
                high[at : at + 16, :] = h
                low[at : at + 16, :] = l
    for t in range(4):
        at = slice(t * 256, (t + 1) * 256)
        value = mul3((high[...], low[...]), (block_high[:, at], block_low[:, at]))
        for m in range(8):
            for half in range(2):
                at = (2 * t + half) * 64
                out[m, at : at + 64, :] = value[m * 64 : (m + 1) * 64, half * 128 : (half + 1) * 128]
    cross = mul3(split(own_ref[...]), (high[:256], low[:256]), mul_nt)
    for m in range(8):
        out[m, 512:528, :] = cross[:, :128]
        out[m, 528:544, :] = cross[:, 128:]


def near_kernel(parts, out):
    total = ((parts[0] + parts[1]) + (parts[2] + parts[3])) + ((parts[4] + parts[5]) + (parts[6] + parts[7]))
    for m in range(4):
        out[m, :128, :] = total[m * 128 : (m + 1) * 128]
        out[m, 128:, :] = total[512:]


def far_kernel(parts, out, cross):
    total = (parts[0] + parts[1]) + (parts[2] + parts[3])
    for m in range(4):
        out[m] = total[:128]
    cross[:, :128] = total[128:144]
    cross[:, 128:] = total[144:]


def copy_kernel(share, out, sems):
    copies = [pltpu.make_async_copy(share, out.at[m], sems.at[m]) for m in range(8)]
    for copy in copies:
        copy.start()
    for copy in copies:
        copy.wait()


def weight_kernel(second_ref, first_ref, out):
    for panel, ref in enumerate((second_ref, first_ref)):
        out[0, :, panel * 256 : (panel + 1) * 256], out[1, :, panel * 256 : (panel + 1) * 256] = split(ref[...].T)


def update_kernel(block, w_ref, parts_ref, out_ref, parts, high, low, out, reads, writes):
    loads = [pltpu.make_async_copy(parts_ref.at[m], parts.at[m], reads.at[m]) for m in range(8)]
    for load in loads:
        load.start()
    for m in range(8):
        loads[m].wait()
        rows = slice(m * 64, (m + 1) * 64)
        high[rows], low[rows] = split(jnp.concatenate([parts[m, j * 64 : (j + 1) * 64] for j in range(8)], axis=1))
    stores = []
    for t in range(4):
        rows = slice(t * 128, (t + 1) * 128)
        change = mul3((w_ref[0, rows], w_ref[1, rows]), (high[...], low[...]))
        out[rows] = block[rows] - change
        stores.append(pltpu.make_async_copy(out.at[rows], out_ref.at[rows], writes.at[t]))
        stores[t].start()
    for store in stores:
        store.wait()


def call(kernel, outs, args, scratch=(), scalars=0, inputs=None, out_spec=VMEM, limit=48):
    single = not isinstance(outs, list)
    return pl.pallas_call(
        kernel,
        out_shape=outs,
        in_specs=inputs or [SMEM] * scalars + [VMEM] * (len(args) - scalars),
        out_specs=out_spec if single else [out_spec] * len(outs),
        scratch_shapes=list(scratch),
        compiler_params=pltpu.CompilerParams(vmem_limit_bytes=limit * 2**20),
    )(*args)


def shape(*dims, dtype=F32):
    return jax.ShapeDtypeStruct(dims, dtype)


def exact(left, right):
    dims = (((0,), (0,)), ((), ()))
    return lax.dot_general(left, right, dims, precision=lax.Precision.HIGHEST, preferred_element_type=F32)


def trade(pieces, groups):
    return lax.all_to_all(pieces, ROW + COL, 0, 0, axis_index_groups=groups)


def local(vectors, reflectors_first, reflectors_second, factor_first, factor_second):
    core = lax.axis_index("core")
    shards = jnp.concatenate([reflectors_second, reflectors_first], axis=0)
    mine = lax.all_to_all(jnp.broadcast_to(shards[None], (NZ,) + shards.shape), "z", 0, 0)
    other = lax.ppermute(mine, "core", [(0, 1), (1, 0)])
    wide = pltpu.VMEM((512, 512), BF16)
    block = call(split_kernel, [shape(512, 1024, dtype=BF16)] * 2, (vectors,))
    parts = call(
        project_kernel,
        shape(8, 544, 128),
        (core.astype(jnp.int32).reshape(1), mine, other, reflectors_first, *block),
        (wide, wide, pltpu.VMEM((2, 8, 32, 512), F32)),
        scalars=1,
    )
    parts = call(near_kernel, shape(4, 160, 128), (trade(parts, NEAR),))
    share, cross = call(far_kernel, [shape(4, 128, 128), shape(16, 256)], (trade(parts, FAR),))
    share = trade(share, FAR).reshape(512, 128)
    copies = call(copy_kernel, shape(8, 512, 128), (share,), (pltpu.SemaphoreType.DMA((8,)),), out_spec=HBM)
    proj = trade(copies, NEAR)
    cross = lax.all_gather(cross, COL, axis=0, tiled=True)
    by_core = jnp.stack([jnp.where(core == 0, mine, other), jnp.where(core == 0, other, mine)], axis=1)
    second = by_core[:, :, :16].reshape(256, 512)
    first = by_core[:, :, 16:].reshape(256, 512)
    w_first = exact(factor_first, first)
    w_second = exact(factor_second, second - exact(cross, w_first))
    weights = call(weight_kernel, shape(2, 512, 512, dtype=BF16), (w_second, w_first))
    tall = pltpu.VMEM((512, 1024), BF16)
    return call(
        update_kernel,
        shape(512, 1024),
        (vectors, weights, proj),
        (
            pltpu.VMEM((8, 512, 128), F32),
            tall,
            tall,
            pltpu.VMEM((512, 1024), F32),
            pltpu.SemaphoreType.DMA((8,)),
            pltpu.SemaphoreType.DMA((4,)),
        ),
        inputs=[VMEM, VMEM, HBM],
        out_spec=HBM,
    )


def solution(mesh):
    fine = Mesh(mesh.devices.reshape(NX, NY, NZ, 2), ROW + COL)
    return jax.shard_map(
        local,
        mesh=fine,
        in_specs=(P(ROW, COL), P(COL, ROW), P(COL, ROW), P(), P()),
        out_specs=P(ROW, COL),
        check_vma=False,
    )
```

```python
import jax
import jax.numpy as jnp
from jax import lax
from jax.experimental import pallas as pl
from jax.experimental.pallas import tpu as pltpu
from jax.sharding import Mesh, PartitionSpec as P

ROW = ("x", "y")
COL = ("z", "core")
NX, NY, NZ = 4, 8, 8
F32, BF16 = jnp.float32, jnp.bfloat16
VMEM = pl.BlockSpec(memory_space=pltpu.VMEM)
SMEM = pl.BlockSpec(memory_space=pltpu.SMEM)
HBM = pl.BlockSpec(memory_space=pltpu.HBM)
PARAMS = pltpu.CompilerParams(vmem_limit_bytes=48 * 2**20)


def device(x, y, z, core):
    return ((x % NX * NY + y % NY) * NZ + z) * 2 + core


NEAR = [
    [device(bx + (px ^ core) + core, by + (py ^ core) + core, z, core) for px in range(2) for py in range(2)]
    for z in range(NZ)
    for core in range(2)
    for bx in range(0, NX, 2)
    for by in range(0, NY, 2)
]
FAR = [
    [device(px + dx, py + dy, z, core) for dx in range(0, NX, 2) for dy in range(0, NY, 2)]
    for z in range(NZ)
    for core in range(2)
    for px in range(2)
    for py in range(2)
]


def split(value):
    high = value.astype(BF16)
    return high, (value - high.astype(F32)).astype(BF16)


def mul(a, b):
    return jnp.dot(a, b, preferred_element_type=F32)


def mul_nt(a, b):
    return lax.dot_general(a, b, (((1,), (1,)), ((), ())), preferred_element_type=F32)


def mul3(a, b, mul=mul):
    return mul(a[0], b[0]) + (mul(a[0], b[1]) + mul(a[1], b[0]))


def split_kernel(block_ref, high, low):
    high[...], low[...] = split(block_ref[...])


def mine_kernel(mine_ref, block_high, block_low, out):
    out[...] = mul3(split(mine_ref[...]), (block_high[...], block_low[...]))


def other_kernel(core_ref, mine_ref, other_ref, own_ref, proj_ref, block_high, block_low, out, both, second):
    other = split(other_ref[...])
    for t in range(4):
        at = slice(t * 256, (t + 1) * 256)
        proj = mul3(other, (block_high[:, at], block_low[:, at]))
        for half in range(2):
            to = slice((2 * t + half) * 128, (2 * t + half + 1) * 128)
            at = slice(half * 128, (half + 1) * 128)
            for m in range(2):
                out[m, to, :] = proj_ref[m * 128 : (m + 1) * 128, to]
                out[2 + m, to, :] = proj[m * 128 : (m + 1) * 128, at]
    core = core_ref[0]
    both[0] = mine_ref[...]
    both[1] = other_ref[...]
    for c in range(2):
        from_core = both.at[core ^ c]
        for z in range(8):
            second[z * 32 + c * 16 : z * 32 + c * 16 + 16, :] = from_core[z * 32 : z * 32 + 16, :]
    cross = mul3(split(own_ref[...]), split(second[...]), mul_nt)
    for m in range(4):
        out[m, 1024:1040, :] = cross[:, :128]
        out[m, 1040:, :] = cross[:, 128:]


def near_kernel(parts, out):
    total = (parts[0] + parts[1]) + (parts[2] + parts[3])
    for m in range(8):
        out[m, :128, :] = total[m * 128 : (m + 1) * 128]
        out[m, 128:, :] = total[1024:]


def far_kernel(parts, out, cross):
    total = ((parts[0] + parts[1]) + (parts[2] + parts[3])) + ((parts[4] + parts[5]) + (parts[6] + parts[7]))
    for m in range(8):
        out[m] = total[:128]
    cross[:, :128] = total[128:144]
    cross[:, 128:] = total[144:]


def pass_kernel(share, after, out):
    out[...] = share[...]


ORDER = (0, 2, 1, 3)


def weight_kernel(core_ref, j_ref, second_ref, first_ref, out, rows, ordered):
    core, j = core_ref[0], j_ref[0]
    for c in range(2):
        for z in range(8):
            at = pl.ds(pl.multiple_of(z * 32 + (core ^ c) * 16, 16), 16)
            to = c * 256 + z * 32
            rows[to : to + 16, :] = second_ref[at, :]
            rows[to + 16 : to + 32, :] = first_ref[at, :]
    for place, d in enumerate(ORDER):
        ordered[place * 128 : (place + 1) * 128, :] = rows[pl.ds(pl.multiple_of((j ^ d) * 128, 128), 128), :]
    out[0], out[1] = split(ordered[...].T)


def natural(parts):
    return jnp.concatenate(
        [jnp.concatenate([part[t * 128 : (t + 1) * 128, :] for t in range(8)], axis=1) for part in parts], axis=0
    )


def middle_kernel(block, w_ref, own, got, out):
    proj = split(natural((own, got)))
    for t in range(2):
        rows = slice(t * 256, (t + 1) * 256)
        out[rows] = block[rows] - mul3((w_ref[0, rows, :256], w_ref[1, rows, :256]), proj)


def update_kernel(middle, w_ref, got, last, out_ref, out, sems):
    proj = split(natural((got, last)))
    stores = []
    for t in range(4):
        rows = slice(t * 128, (t + 1) * 128)
        out[rows] = middle[rows] - mul3((w_ref[0, rows, 256:], w_ref[1, rows, 256:]), proj)
        stores.append(pltpu.make_async_copy(out.at[rows], out_ref.at[rows], sems.at[t]))
        stores[t].start()
    for store in stores:
        store.wait()


def call(kernel, outs, args, scratch=(), scalars=0, inputs=None, out_spec=VMEM):
    single = not isinstance(outs, list)
    return pl.pallas_call(
        kernel,
        out_shape=outs,
        in_specs=inputs or [SMEM] * scalars + [VMEM] * (len(args) - scalars),
        out_specs=out_spec if single else [out_spec] * len(outs),
        scratch_shapes=list(scratch),
        compiler_params=PARAMS,
    )(*args)


def shape(*dims, dtype=F32):
    return jax.ShapeDtypeStruct(dims, dtype)


def exact(left, right):
    dims = (((0,), (0,)), ((), ()))
    return lax.dot_general(left, right, dims, precision=lax.Precision.HIGHEST, preferred_element_type=F32)


def trade(pieces, groups):
    return lax.all_to_all(pieces, ROW + COL, 0, 0, axis_index_groups=groups)


def fetch(value, d):
    def partner(i, n, core):
        return (i + 1) % n if i % 2 == core else (i - 1) % n

    pairs = [
        (device(x, y, z, c), device(partner(x, NX, c) if d & 2 else x, partner(y, NY, c) if d & 1 else y, z, c))
        for x in range(NX)
        for y in range(NY)
        for z in range(NZ)
        for c in range(2)
    ]
    return lax.ppermute(value, ROW + COL, pairs)


def local(vectors, reflectors_first, reflectors_second, factor_first, factor_second):
    core = lax.axis_index("core")
    scalar = core.astype(jnp.int32).reshape(1)
    j = ((lax.axis_index("x") % 2) * 2 + lax.axis_index("y") % 2).astype(jnp.int32).reshape(1)
    shards = jnp.concatenate([reflectors_second, reflectors_first], axis=0)
    mine = lax.all_to_all(jnp.broadcast_to(shards[None], (NZ,) + shards.shape), "z", 0, 0).reshape(256, 512)
    other = lax.ppermute(mine, "core", [(0, 1), (1, 0)])
    block = call(split_kernel, [shape(512, 1024, dtype=BF16)] * 2, (vectors,))
    proj = call(mine_kernel, shape(256, 1024), (mine, *block))
    parts = call(
        other_kernel,
        shape(4, 1056, 128),
        (scalar, mine, other, reflectors_first, proj, *block),
        (pltpu.VMEM((2, 256, 512), F32), pltpu.VMEM((256, 512), F32)),
        scalars=1,
    )
    parts = call(near_kernel, shape(8, 160, 128), (trade(parts, NEAR),))
    share, cross = call(far_kernel, [shape(8, 128, 128), shape(16, 256)], (trade(parts, FAR),))
    share = trade(share, FAR).reshape(1024, 128)
    cross = lax.all_gather(cross, COL, axis=0, tiled=True)
    share = call(pass_kernel, shape(1024, 128), (share, cross), inputs=[VMEM, HBM])
    got = {d: fetch(share, d) for d in (3, 2, 1)}
    both = jnp.stack([jnp.where(core == 0, mine, other), jnp.where(core == 0, other, mine)]).reshape(2, 8, 32, 512)
    by_core = both.transpose(1, 0, 2, 3)
    second = by_core[:, :, :16].reshape(256, 512)
    first = by_core[:, :, 16:].reshape(256, 512)
    w_first = exact(factor_first, first)
    w_second = exact(factor_second, second - exact(cross, w_first))
    square = pltpu.VMEM((512, 512), F32)
    weights = call(
        weight_kernel, shape(2, 512, 512, dtype=BF16), (scalar, j, w_second, w_first), (square, square), scalars=2
    )
    middle = call(middle_kernel, shape(512, 1024), (vectors, weights, share, got[2]))
    return call(
        update_kernel,
        shape(512, 1024),
        (middle, weights, got[1], got[3]),
        (pltpu.VMEM((512, 1024), F32), pltpu.SemaphoreType.DMA((4,))),
        out_spec=HBM,
    )


def solution(mesh):
    fine = Mesh(mesh.devices.reshape(NX, NY, NZ, 2), ROW + COL)
    return jax.shard_map(
        local,
        mesh=fine,
        in_specs=(P(ROW, COL), P(COL, ROW), P(COL, ROW), P(), P()),
        out_specs=P(ROW, COL),
        check_vma=False,
    )
```

```python
import jax
import jax.numpy as jnp
from jax import lax
from jax.experimental import pallas as pl
from jax.experimental.pallas import tpu as pltpu
from jax.sharding import Mesh, PartitionSpec as P

ROW = ("x", "y")
COL = ("z", "core")
NX, NY, NZ = 4, 8, 8
F32, BF16 = jnp.float32, jnp.bfloat16
VMEM = pl.BlockSpec(memory_space=pltpu.VMEM)
SMEM = pl.BlockSpec(memory_space=pltpu.SMEM)
HBM = pl.BlockSpec(memory_space=pltpu.HBM)
PARAMS = pltpu.CompilerParams(vmem_limit_bytes=48 * 2**20)


def device(x, y, z, core):
    return ((x % NX * NY + y % NY) * NZ + z) * 2 + core


NEAR = [
    [device(bx + (px ^ core) + core, by + (py ^ core) + core, z, core) for px in range(2) for py in range(2)]
    for z in range(NZ)
    for core in range(2)
    for bx in range(0, NX, 2)
    for by in range(0, NY, 2)
]
FAR = [
    [device(px + dx, py + dy, z, core) for dx in range(0, NX, 2) for dy in range(0, NY, 2)]
    for z in range(NZ)
    for core in range(2)
    for px in range(2)
    for py in range(2)
]


def split(value):
    high = value.astype(BF16)
    return high, (value - high.astype(F32)).astype(BF16)


def mul(a, b):
    return jnp.dot(a, b, preferred_element_type=F32)


def mul_nt(a, b):
    return lax.dot_general(a, b, (((1,), (1,)), ((), ())), preferred_element_type=F32)


def mul3(a, b, mul=mul):
    return mul(a[0], b[0]) + (mul(a[0], b[1]) + mul(a[1], b[0]))


def shard_kernel(second, first, out):
    for z in range(8):
        out[z, :16] = second[...]
        out[z, 16:] = first[...]


def split_kernel(block_ref, high, low):
    high[...], low[...] = split(block_ref[...])


def project_kernel(core_ref, mine_ref, other_ref, own_ref, block_high, block_low, out, high, low, both):
    core = core_ref[0]
    both[0] = mine_ref[...]
    both[1] = other_ref[...]
    for c in range(2):
        from_core = both.at[core ^ c]
        for z in range(8):
            for panel in range(2):
                h, l = split(from_core[z, panel * 16 : panel * 16 + 16, :])
                at = panel * 256 + z * 32 + c * 16
                high[at : at + 16, :] = h
                low[at : at + 16, :] = l
    for t in range(4):
        at = slice(t * 256, (t + 1) * 256)
        value = mul3((high[...], low[...]), (block_high[:, at], block_low[:, at]))
        for m in range(4):
            for half in range(2):
                to = (2 * t + half) * 128
                out[m, to : to + 128, :] = value[m * 128 : (m + 1) * 128, half * 128 : (half + 1) * 128]
    cross = mul3(split(own_ref[...]), (high[:256], low[:256]), mul_nt)
    for m in range(4):
        out[m, 1024:1040, :] = cross[:, :128]
        out[m, 1040:, :] = cross[:, 128:]


def near_kernel(parts, out):
    total = (parts[0] + parts[1]) + (parts[2] + parts[3])
    for m in range(8):
        out[m, :128, :] = total[m * 128 : (m + 1) * 128]
        out[m, 128:, :] = total[1024:]


def far_kernel(parts, after, out, cross):
    total = ((parts[0] + parts[1]) + (parts[2] + parts[3])) + ((parts[4] + parts[5]) + (parts[6] + parts[7]))
    for m in range(8):
        out[m] = total[:128]
    cross[:, :128] = total[128:144]
    cross[:, 128:] = total[144:]


def pass_kernel(share, after, out):
    out[...] = share[...]


ORDER = (0, 3, 2, 1)


def weight_kernel(j_ref, second_ref, first_ref, out, ordered):
    j = j_ref[0]
    for place, d in enumerate(ORDER):
        quarter = j ^ d
        at = pl.ds(pl.multiple_of((quarter & 1) * 128, 128), 128)
        rows = jnp.where(quarter < 2, second_ref[at, :], first_ref[at, :])
        ordered[place * 128 : (place + 1) * 128, :] = rows
    out[0], out[1] = split(ordered[...].T)


def natural(parts):
    return jnp.concatenate(
        [jnp.concatenate([part[t * 128 : (t + 1) * 128, :] for t in range(8)], axis=1) for part in parts], axis=0
    )


def middle_kernel(block, w_ref, own, got, out):
    proj = split(natural((own, got)))
    for t in range(2):
        rows = slice(t * 256, (t + 1) * 256)
        out[rows] = block[rows] - mul3((w_ref[0, rows, :256], w_ref[1, rows, :256]), proj)


def update_kernel(middle, w_ref, got, last, out_ref, out, sems):
    proj = split(natural((got, last)))
    stores = []
    for t in range(4):
        rows = slice(t * 128, (t + 1) * 128)
        out[rows] = middle[rows] - mul3((w_ref[0, rows, 256:], w_ref[1, rows, 256:]), proj)
        stores.append(pltpu.make_async_copy(out.at[rows], out_ref.at[rows], sems.at[t]))
        stores[t].start()
    for store in stores:
        store.wait()


def call(kernel, outs, args, scratch=(), scalars=0, inputs=None, out_spec=VMEM):
    single = not isinstance(outs, list)
    return pl.pallas_call(
        kernel,
        out_shape=outs,
        in_specs=inputs or [SMEM] * scalars + [VMEM] * (len(args) - scalars),
        out_specs=out_spec if single else [out_spec] * len(outs),
        scratch_shapes=list(scratch),
        compiler_params=PARAMS,
    )(*args)


def shape(*dims, dtype=F32):
    return jax.ShapeDtypeStruct(dims, dtype)


def exact(left, right):
    dims = (((0,), (0,)), ((), ()))
    return lax.dot_general(left, right, dims, precision=lax.Precision.HIGHEST, preferred_element_type=F32)


def trade(pieces, groups):
    return lax.all_to_all(pieces, ROW + COL, 0, 0, axis_index_groups=groups)


def fetch(value, d):
    def partner(i, n, core):
        return (i + 1) % n if i % 2 == core else (i - 1) % n

    pairs = [
        (device(x, y, z, c), device(partner(x, NX, c) if d & 2 else x, partner(y, NY, c) if d & 1 else y, z, c))
        for x in range(NX)
        for y in range(NY)
        for z in range(NZ)
        for c in range(2)
    ]
    return lax.ppermute(value, ROW + COL, pairs)


def local(vectors, reflectors_first, reflectors_second, factor_first, factor_second):
    core = lax.axis_index("core")
    scalar = core.astype(jnp.int32).reshape(1)
    j = ((lax.axis_index("x") % 2) * 2 + lax.axis_index("y") % 2).astype(jnp.int32).reshape(1)
    shards = call(shard_kernel, shape(NZ, 32, 512), (reflectors_second, reflectors_first))
    mine = lax.all_to_all(shards, "z", 0, 0)
    other = lax.ppermute(mine, "core", [(0, 1), (1, 0)])
    block = call(split_kernel, [shape(512, 1024, dtype=BF16)] * 2, (vectors,))
    wide = pltpu.VMEM((512, 512), BF16)
    parts = call(
        project_kernel,
        shape(4, 1056, 128),
        (scalar, mine, other, reflectors_first, *block),
        (wide, wide, pltpu.VMEM((2, 8, 32, 512), F32)),
        scalars=1,
    )
    by_core = jnp.stack([jnp.where(core == 0, mine, other), jnp.where(core == 0, other, mine)], axis=1)
    second = by_core[:, :, :16].reshape(256, 512)
    first = by_core[:, :, 16:].reshape(256, 512)
    w_first = exact(factor_first, first)
    parts = call(near_kernel, shape(8, 160, 128), (trade(parts, NEAR),))
    share, cross = call(
        far_kernel, [shape(8, 128, 128), shape(16, 256)], (trade(parts, FAR), w_first), inputs=[VMEM, HBM]
    )
    share = trade(share, FAR).reshape(1024, 128)
    cross = lax.all_gather(cross, COL, axis=0, tiled=True)
    share = call(pass_kernel, shape(1024, 128), (share, cross), inputs=[VMEM, HBM])
    got = {d: fetch(share, d) for d in (3, 2, 1)}
    w_second = exact(factor_second, second - exact(cross, w_first))
    weights = call(
        weight_kernel,
        shape(2, 512, 512, dtype=BF16),
        (j, w_second, w_first),
        (pltpu.VMEM((512, 512), F32),),
        scalars=1,
    )
    middle = call(middle_kernel, shape(512, 1024), (vectors, weights, share, got[3]))
    return call(
        update_kernel,
        shape(512, 1024),
        (middle, weights, got[2], got[1]),
        (pltpu.VMEM((512, 1024), F32), pltpu.SemaphoreType.DMA((4,))),
        out_spec=HBM,
    )


def solution(mesh):
    fine = Mesh(mesh.devices.reshape(NX, NY, NZ, 2), ROW + COL)
    return jax.shard_map(
        local,
        mesh=fine,
        in_specs=(P(ROW, COL), P(COL, ROW), P(COL, ROW), P(), P()),
        out_specs=P(ROW, COL),
        check_vma=False,
    )
```

```python
import jax
import jax.numpy as jnp
from jax import lax
from jax.experimental import pallas as pl
from jax.experimental.pallas import tpu as pltpu
from jax.sharding import Mesh, PartitionSpec as P

ROW = ("x", "y")
COL = ("z", "core")
NX, NY, NZ = 4, 8, 8
F32, BF16 = jnp.float32, jnp.bfloat16
VMEM = pl.BlockSpec(memory_space=pltpu.VMEM)
SMEM = pl.BlockSpec(memory_space=pltpu.SMEM)
HBM = pl.BlockSpec(memory_space=pltpu.HBM)
PARAMS = pltpu.CompilerParams(vmem_limit_bytes=48 * 2**20)


def device(x, y, z, core):
    return ((x % NX * NY + y % NY) * NZ + z) * 2 + core


FAR = [
    [device(px + dx, py + dy, z, core) for dx in range(0, NX, 2) for dy in range(0, NY, 2)]
    for z in range(NZ)
    for core in range(2)
    for px in range(2)
    for py in range(2)
]


def split(value):
    high = value.astype(BF16)
    return high, (value - high.astype(F32)).astype(BF16)


def mul(a, b):
    return jnp.dot(a, b, preferred_element_type=F32)


def mul_nt(a, b):
    return lax.dot_general(a, b, (((1,), (1,)), ((), ())), preferred_element_type=F32)


def mul3(a, b, mul=mul):
    return mul(a[0], b[0]) + (mul(a[0], b[1]) + mul(a[1], b[0]))


def split_kernel(block_ref, high, low):
    high[...], low[...] = split(block_ref[...])


def quarter(rows, block_high, block_low, out):
    for t in range(4):
        at = slice(t * 256, (t + 1) * 256)
        value = mul3(rows, (block_high[:, at], block_low[:, at]))
        for half in range(2):
            to = (2 * t + half) * 128
            out[to : to + 128, :] = value[:, half * 128 : (half + 1) * 128]


def rows_of(j, d, high, low):
    at = pl.ds(pl.multiple_of((j ^ d) * 128, 128), 128)
    return high[at, :], low[at, :]


def diagonal_kernel(core_ref, j_ref, mine_ref, other_ref, own_ref, block_high, block_low, out, high, low, both):
    core = core_ref[0]
    both[0] = mine_ref[...]
    both[1] = other_ref[...]
    for c in range(2):
        from_core = both.at[core ^ c]
        for z in range(8):
            for panel in range(2):
                h, l = split(from_core[z, panel * 16 : panel * 16 + 16, :])
                at = panel * 256 + z * 32 + c * 16
                high[at : at + 16, :] = h
                low[at : at + 16, :] = l
    quarter(rows_of(j_ref[0], 3, high, low), block_high, block_low, out)
    cross = mul3(split(own_ref[...]), (high[:256], low[:256]), mul_nt)
    out[1024:1040, :] = cross[:, :128]
    out[1040:, :] = cross[:, 128:]


def beside_kernel(j_ref, diagonal, high, low, block_high, block_low, *outs):
    for d, out in zip((2, 1), outs):
        quarter(rows_of(j_ref[0], d, high, low), block_high, block_low, out)
        out[1024:, :] = diagonal[1024:, :]


def own_kernel(j_ref, diagonal, got, high, low, block_high, block_low, out):
    quarter(rows_of(j_ref[0], 0, high, low), block_high, block_low, out)
    out[1024:, :] = diagonal[1024:, :]
    out[...] += got[...]


def near_kernel(half, got1, got2, out):
    total = half[...] + (got1[...] + got2[...])
    for m in range(8):
        out[m, :128, :] = total[m * 128 : (m + 1) * 128]
        out[m, 128:, :] = total[1024:]


def far_kernel(parts, after, out, cross):
    total = ((parts[0] + parts[1]) + (parts[2] + parts[3])) + ((parts[4] + parts[5]) + (parts[6] + parts[7]))
    for m in range(8):
        out[m] = total[:128]
    cross[:, :128] = total[128:144]
    cross[:, 128:] = total[144:]


def pass_kernel(share, after, out):
    out[...] = share[...]


ORDER = (0, 3, 2, 1)


def weight_kernel(j_ref, second_ref, first_ref, out, ordered):
    j = j_ref[0]
    for place, d in enumerate(ORDER):
        quarter = j ^ d
        at = pl.ds(pl.multiple_of((quarter & 1) * 128, 128), 128)
        rows = jnp.where(quarter < 2, second_ref[at, :], first_ref[at, :])
        ordered[place * 128 : (place + 1) * 128, :] = rows
    out[0], out[1] = split(ordered[...].T)


def natural(parts):
    return jnp.concatenate(
        [jnp.concatenate([part[t * 128 : (t + 1) * 128, :] for t in range(8)], axis=1) for part in parts], axis=0
    )


def middle_kernel(block, w_ref, own, got, out):
    proj = split(natural((own, got)))
    for t in range(2):
        rows = slice(t * 256, (t + 1) * 256)
        out[rows] = block[rows] - mul3((w_ref[0, rows, :256], w_ref[1, rows, :256]), proj)


def update_kernel(middle, w_ref, got, last, out_ref, out, sems):
    proj = split(natural((got, last)))
    stores = []
    for t in range(4):
        rows = slice(t * 128, (t + 1) * 128)
        out[rows] = middle[rows] - mul3((w_ref[0, rows, 256:], w_ref[1, rows, 256:]), proj)
        stores.append(pltpu.make_async_copy(out.at[rows], out_ref.at[rows], sems.at[t]))
        stores[t].start()
    for store in stores:
        store.wait()


def call(kernel, outs, args, scratch=(), scalars=0, inputs=None, out_spec=VMEM):
    single = not isinstance(outs, list)
    return pl.pallas_call(
        kernel,
        out_shape=outs,
        in_specs=inputs or [SMEM] * scalars + [VMEM] * (len(args) - scalars),
        out_specs=out_spec if single else [out_spec] * len(outs),
        scratch_shapes=list(scratch),
        compiler_params=PARAMS,
    )(*args)


def shape(*dims, dtype=F32):
    return jax.ShapeDtypeStruct(dims, dtype)


def exact(left, right):
    dims = (((0,), (0,)), ((), ()))
    return lax.dot_general(left, right, dims, precision=lax.Precision.HIGHEST, preferred_element_type=F32)


def trade(pieces):
    return lax.all_to_all(pieces, ROW + COL, 0, 0, axis_index_groups=FAR)


def fetch(value, d):
    def partner(i, n, core):
        return (i + 1) % n if i % 2 == core else (i - 1) % n

    pairs = [
        (device(x, y, z, c), device(partner(x, NX, c) if d & 2 else x, partner(y, NY, c) if d & 1 else y, z, c))
        for x in range(NX)
        for y in range(NY)
        for z in range(NZ)
        for c in range(2)
    ]
    return lax.ppermute(value, ROW + COL, pairs)


def local(vectors, reflectors_first, reflectors_second, factor_first, factor_second):
    core = lax.axis_index("core")
    scalar = core.astype(jnp.int32).reshape(1)
    j = ((lax.axis_index("x") % 2) * 2 + lax.axis_index("y") % 2).astype(jnp.int32).reshape(1)
    shards = jnp.concatenate([reflectors_second, reflectors_first], axis=0)
    mine = lax.all_to_all(jnp.broadcast_to(shards[None], (NZ,) + shards.shape), "z", 0, 0)
    other = lax.ppermute(mine, "core", [(0, 1), (1, 0)])
    block = call(split_kernel, [shape(512, 1024, dtype=BF16)] * 2, (vectors,))
    wide = shape(512, 512, dtype=BF16)
    diagonal, *panels = call(
        diagonal_kernel,
        [shape(1056, 128), wide, wide],
        (scalar, j, mine, other, reflectors_first, *block),
        (pltpu.VMEM((2, 8, 32, 512), F32),),
        scalars=2,
    )
    along_x, along_y = call(beside_kernel, [shape(1056, 128)] * 2, (j, diagonal, *panels, *block), scalars=1)
    half = call(own_kernel, shape(1056, 128), (j, diagonal, fetch(diagonal, 3), *panels, *block), scalars=1)
    by_core = jnp.stack([jnp.where(core == 0, mine, other), jnp.where(core == 0, other, mine)], axis=1)
    second = by_core[:, :, :16].reshape(256, 512)
    first = by_core[:, :, 16:].reshape(256, 512)
    w_first = exact(factor_first, first)
    parts = call(near_kernel, shape(8, 160, 128), (half, fetch(along_y, 1), fetch(along_x, 2)))
    share, cross = call(
        far_kernel, [shape(8, 128, 128), shape(16, 256)], (trade(parts), w_first), inputs=[VMEM, HBM]
    )
    share = trade(share).reshape(1024, 128)
    cross = lax.all_gather(cross, COL, axis=0, tiled=True)
    share = call(pass_kernel, shape(1024, 128), (share, cross), inputs=[VMEM, HBM])
    got = {d: fetch(share, d) for d in (3, 2, 1)}
    w_second = exact(factor_second, second - exact(cross, w_first))
    weights = call(
        weight_kernel,
        shape(2, 512, 512, dtype=BF16),
        (j, w_second, w_first),
        (pltpu.VMEM((512, 512), F32),),
        scalars=1,
    )
    middle = call(middle_kernel, shape(512, 1024), (vectors, weights, share, got[3]))
    return call(
        update_kernel,
        shape(512, 1024),
        (middle, weights, got[2], got[1]),
        (pltpu.VMEM((512, 1024), F32), pltpu.SemaphoreType.DMA((4,))),
        out_spec=HBM,
    )


def solution(mesh):
    fine = Mesh(mesh.devices.reshape(NX, NY, NZ, 2), ROW + COL)
    return jax.shard_map(
        local,
        mesh=fine,
        in_specs=(P(ROW, COL), P(COL, ROW), P(COL, ROW), P(), P()),
        out_specs=P(ROW, COL),
        check_vma=False,
    )
```

```python
import jax
import jax.numpy as jnp
from jax import lax
from jax.experimental import pallas as pl
from jax.experimental.pallas import tpu as pltpu
from jax.sharding import Mesh, PartitionSpec as P

ROW = ("x", "y")
COL = ("z", "core")
NX, NY, NZ = 4, 8, 8
F32, BF16 = jnp.float32, jnp.bfloat16
VMEM = pl.BlockSpec(memory_space=pltpu.VMEM)
SMEM = pl.BlockSpec(memory_space=pltpu.SMEM)
HBM = pl.BlockSpec(memory_space=pltpu.HBM)
PARAMS = pltpu.CompilerParams(vmem_limit_bytes=48 * 2**20)


def device(x, y, z, core):
    return ((x % NX * NY + y % NY) * NZ + z) * 2 + core


def label_x(x, core):
    return (x >> 1) ^ (x & 1 & ~core)


def label_y(y, core):
    y = (y - core) & 7
    return (y & 1) ^ (y >> 2)


FAR = [
    [
        device(x, y, z, core)
        for x in range(NX)
        for y in range(NY)
        if (label_x(x, core), label_y(y, core)) == (px, py)
    ]
    for z in range(NZ)
    for core in range(2)
    for px in range(2)
    for py in range(2)
]


def split(value):
    high = value.astype(BF16)
    return high, (value - high.astype(F32)).astype(BF16)


def mul(a, b):
    return jnp.dot(a, b, preferred_element_type=F32)


def mul_nt(a, b):
    return lax.dot_general(a, b, (((1,), (1,)), ((), ())), preferred_element_type=F32)


def mul3(a, b, mul=mul):
    return mul(a[0], b[0]) + (mul(a[0], b[1]) + mul(a[1], b[0]))


def split_kernel(block_ref, high, low):
    high[...], low[...] = split(block_ref[...])


def quarter(rows, block_high, block_low, out):
    for t in range(4):
        at = slice(t * 256, (t + 1) * 256)
        value = mul3(rows, (block_high[:, at], block_low[:, at]))
        for half in range(2):
            to = (2 * t + half) * 128
            out[to : to + 128, :] = value[:, half * 128 : (half + 1) * 128]


def rows_of(j, d, high, low):
    at = pl.ds(pl.multiple_of((j ^ d) * 128, 128), 128)
    return high[at, :], low[at, :]


def diagonal_kernel(core_ref, j_ref, mine_ref, other_ref, own_ref, block_high, block_low, out, high, low, both):
    core = core_ref[0]
    both[0] = mine_ref[...]
    both[1] = other_ref[...]
    for c in range(2):
        from_core = both.at[core ^ c]
        for z in range(8):
            for panel in range(2):
                h, l = split(from_core[z, panel * 16 : panel * 16 + 16, :])
                at = panel * 256 + z * 32 + c * 16
                high[at : at + 16, :] = h
                low[at : at + 16, :] = l
    quarter(rows_of(j_ref[0], 3, high, low), block_high, block_low, out)
    cross = mul3(split(own_ref[...]), (high[:256], low[:256]), mul_nt)
    out[1024:1040, :] = cross[:, :128]
    out[1040:, :] = cross[:, 128:]


def beside_kernel(j_ref, diagonal, high, low, block_high, block_low, *outs):
    for d, out in zip((2, 1), outs):
        quarter(rows_of(j_ref[0], d, high, low), block_high, block_low, out)
        out[1024:, :] = diagonal[1024:, :]


def own_kernel(j_ref, diagonal, got, high, low, block_high, block_low, out):
    quarter(rows_of(j_ref[0], 0, high, low), block_high, block_low, out)
    out[1024:, :] = diagonal[1024:, :]
    out[...] += got[...]


def near_kernel(half, got1, got2, out):
    total = half[...] + (got1[...] + got2[...])
    for m in range(8):
        out[m, :128, :] = total[m * 128 : (m + 1) * 128]
        out[m, 128:, :] = total[1024:]


def far_kernel(parts, after, out, cross):
    total = ((parts[0] + parts[1]) + (parts[2] + parts[3])) + ((parts[4] + parts[5]) + (parts[6] + parts[7]))
    for m in range(8):
        out[m] = total[:128]
    cross[:, :128] = total[128:144]
    cross[:, 128:] = total[144:]


def pass_kernel(share, after, out):
    out[...] = share[...]


ORDER = (0, 3, 2, 1)


def weight_kernel(j_ref, second_ref, first_ref, out, ordered):
    j = j_ref[0]
    for place, d in enumerate(ORDER):
        quarter = j ^ d
        at = pl.ds(pl.multiple_of((quarter & 1) * 128, 128), 128)
        rows = jnp.where(quarter < 2, second_ref[at, :], first_ref[at, :])
        ordered[place * 128 : (place + 1) * 128, :] = rows
    out[0], out[1] = split(ordered[...].T)


def natural(parts):
    return jnp.concatenate(
        [jnp.concatenate([part[t * 128 : (t + 1) * 128, :] for t in range(8)], axis=1) for part in parts], axis=0
    )


def middle_kernel(block, w_ref, own, got, out):
    proj = split(natural((own, got)))
    for t in range(2):
        rows = slice(t * 256, (t + 1) * 256)
        out[rows] = block[rows] - mul3((w_ref[0, rows, :256], w_ref[1, rows, :256]), proj)


def update_kernel(middle, w_ref, got, last, out_ref, out, sems):
    proj = split(natural((got, last)))
    stores = []
    for t in range(4):
        rows = slice(t * 128, (t + 1) * 128)
        out[rows] = middle[rows] - mul3((w_ref[0, rows, 256:], w_ref[1, rows, 256:]), proj)
        stores.append(pltpu.make_async_copy(out.at[rows], out_ref.at[rows], sems.at[t]))
        stores[t].start()
    for store in stores:
        store.wait()


def call(kernel, outs, args, scratch=(), scalars=0, inputs=None, out_spec=VMEM):
    single = not isinstance(outs, list)
    return pl.pallas_call(
        kernel,
        out_shape=outs,
        in_specs=inputs or [SMEM] * scalars + [VMEM] * (len(args) - scalars),
        out_specs=out_spec if single else [out_spec] * len(outs),
        scratch_shapes=list(scratch),
        compiler_params=PARAMS,
    )(*args)


def shape(*dims, dtype=F32):
    return jax.ShapeDtypeStruct(dims, dtype)


def exact(left, right):
    dims = (((0,), (0,)), ((), ()))
    return lax.dot_general(left, right, dims, precision=lax.Precision.HIGHEST, preferred_element_type=F32)


def trade(pieces):
    return lax.all_to_all(pieces, ROW + COL, 0, 0, axis_index_groups=FAR)


def fetch(value, d):
    def partner(i, n, core):
        return (i + 1) % n if i % 2 == core else (i - 1) % n

    pairs = [
        (device(x, y, z, c), device(partner(x, NX, c) if d & 2 else x, partner(y, NY, c) if d & 1 else y, z, c))
        for x in range(NX)
        for y in range(NY)
        for z in range(NZ)
        for c in range(2)
    ]
    return lax.ppermute(value, ROW + COL, pairs)


def local(vectors, reflectors_first, reflectors_second, factor_first, factor_second):
    core = lax.axis_index("core")
    scalar = core.astype(jnp.int32).reshape(1)
    j = label_x(lax.axis_index("x"), core) * 2 + label_y(lax.axis_index("y"), core)
    j = j.astype(jnp.int32).reshape(1)
    shards = jnp.concatenate([reflectors_second, reflectors_first], axis=0)
    mine = lax.all_to_all(jnp.broadcast_to(shards[None], (NZ,) + shards.shape), "z", 0, 0)
    other = lax.ppermute(mine, "core", [(0, 1), (1, 0)])
    block = call(split_kernel, [shape(512, 1024, dtype=BF16)] * 2, (vectors,))
    wide = shape(512, 512, dtype=BF16)
    diagonal, *panels = call(
        diagonal_kernel,
        [shape(1056, 128), wide, wide],
        (scalar, j, mine, other, reflectors_first, *block),
        (pltpu.VMEM((2, 8, 32, 512), F32),),
        scalars=2,
    )
    along_x, along_y = call(beside_kernel, [shape(1056, 128)] * 2, (j, diagonal, *panels, *block), scalars=1)
    half = call(own_kernel, shape(1056, 128), (j, diagonal, fetch(diagonal, 3), *panels, *block), scalars=1)
    by_core = jnp.stack([jnp.where(core == 0, mine, other), jnp.where(core == 0, other, mine)], axis=1)
    second = by_core[:, :, :16].reshape(256, 512)
    first = by_core[:, :, 16:].reshape(256, 512)
    w_first = exact(factor_first, first)
    parts = call(near_kernel, shape(8, 160, 128), (half, fetch(along_y, 1), fetch(along_x, 2)))
    share, cross = call(
        far_kernel, [shape(8, 128, 128), shape(16, 256)], (trade(parts), w_first), inputs=[VMEM, HBM]
    )
    share = trade(share).reshape(1024, 128)
    cross = lax.all_gather(cross, COL, axis=0, tiled=True)
    share = call(pass_kernel, shape(1024, 128), (share, cross), inputs=[VMEM, HBM])
    got = {d: fetch(share, d) for d in (3, 2, 1)}
    w_second = exact(factor_second, second - exact(cross, w_first))
    weights = call(
        weight_kernel,
        shape(2, 512, 512, dtype=BF16),
        (j, w_second, w_first),
        (pltpu.VMEM((512, 512), F32),),
        scalars=1,
    )
    middle = call(middle_kernel, shape(512, 1024), (vectors, weights, share, got[3]))
    return call(
        update_kernel,
        shape(512, 1024),
        (middle, weights, got[2], got[1]),
        (pltpu.VMEM((512, 1024), F32), pltpu.SemaphoreType.DMA((4,))),
        out_spec=HBM,
    )


def solution(mesh):
    fine = Mesh(mesh.devices.reshape(NX, NY, NZ, 2), ROW + COL)
    return jax.shard_map(
        local,
        mesh=fine,
        in_specs=(P(ROW, COL), P(COL, ROW), P(COL, ROW), P(), P()),
        out_specs=P(ROW, COL),
        check_vma=False,
    )
```

```python
import jax
import jax.numpy as jnp
from jax import lax
from jax.experimental import pallas as pl
from jax.experimental.pallas import tpu as pltpu
from jax.sharding import Mesh, PartitionSpec as P

ROW = ("x", "y")
COL = ("z", "core")
NX, NY, NZ = 4, 8, 8
F32, BF16 = jnp.float32, jnp.bfloat16
VMEM = pl.BlockSpec(memory_space=pltpu.VMEM)
SMEM = pl.BlockSpec(memory_space=pltpu.SMEM)
HBM = pl.BlockSpec(memory_space=pltpu.HBM)
PARAMS = pltpu.CompilerParams(vmem_limit_bytes=48 * 2**20)


def device(x, y, z, core):
    return ((x % NX * NY + y % NY) * NZ + z) * 2 + core


def label_x(x, core):
    return (x >> 1) ^ (x & 1 & ~core)


def label_y(y, core):
    y = (y - core) & 7
    return (y & 1) ^ (y >> 2)


FAR = [
    [
        device(x, y, z, core)
        for x in range(NX)
        for y in range(NY)
        if (label_x(x, core), label_y(y, core)) == (px, py)
    ]
    for z in range(NZ)
    for core in range(2)
    for px in range(2)
    for py in range(2)
]


PARITY = [
    [device(x, y, z, core) for x in range(px, NX, 2) for y in range(py, NY, 2)]
    for z in range(NZ)
    for core in range(2)
    for px in range(2)
    for py in range(2)
]


def split(value):
    high = value.astype(BF16)
    return high, (value - high.astype(F32)).astype(BF16)


def mul(a, b):
    return jnp.dot(a, b, preferred_element_type=F32)


def mul_nt(a, b):
    return lax.dot_general(a, b, (((1,), (1,)), ((), ())), preferred_element_type=F32)


def mul3(a, b, mul=mul):
    return mul(a[0], b[0]) + (mul(a[0], b[1]) + mul(a[1], b[0]))


def split_kernel(block_ref, high, low):
    high[...], low[...] = split(block_ref[...])


def quarter(rows, block_high, block_low, out):
    for t in range(4):
        at = slice(t * 256, (t + 1) * 256)
        value = mul3(rows, (block_high[:, at], block_low[:, at]))
        for half in range(2):
            to = (2 * t + half) * 128
            out[to : to + 128, :] = value[:, half * 128 : (half + 1) * 128]


def rows_of(j, d, high, low):
    at = pl.ds(pl.multiple_of((j ^ d) * 128, 128), 128)
    return high[at, :], low[at, :]


def diagonal_kernel(core_ref, j_ref, mine_ref, other_ref, own_ref, block_high, block_low, out, cross_out, high, low, both):
    core = core_ref[0]
    both[0] = mine_ref[...]
    both[1] = other_ref[...]
    for c in range(2):
        from_core = both.at[core ^ c]
        for z in range(8):
            for panel in range(2):
                h, l = split(from_core[z, panel * 16 : panel * 16 + 16, :])
                at = panel * 256 + z * 32 + c * 16
                high[at : at + 16, :] = h
                low[at : at + 16, :] = l
    quarter(rows_of(j_ref[0], 3, high, low), block_high, block_low, out)
    cross = mul3(split(own_ref[...]), (high[:256], low[:256]), mul_nt)
    for m in range(8):
        cross_out[m, :16, :] = cross[:, :128]
        cross_out[m, 16:, :] = cross[:, 128:]


def beside_kernel(j_ref, high, low, block_high, block_low, *outs):
    for d, out in zip((2, 1), outs):
        quarter(rows_of(j_ref[0], d, high, low), block_high, block_low, out)


def own_kernel(j_ref, got, high, low, block_high, block_low, out):
    quarter(rows_of(j_ref[0], 0, high, low), block_high, block_low, out)
    out[...] += got[...]


def sum8(parts):
    return ((parts[0] + parts[1]) + (parts[2] + parts[3])) + ((parts[4] + parts[5]) + (parts[6] + parts[7]))


def cross_kernel(parts, out):
    total = sum8(parts)
    out[:, :128] = total[:16]
    out[:, 128:] = total[16:]


def cross_sum_kernel(own, got1, got2, got3, out):
    out[...] = (own[...] + got1[...]) + (got2[...] + got3[...])


def near_kernel(half, got1, got2, after, out):
    total = half[...] + (got1[...] + got2[...])
    for m in range(8):
        out[m] = total[m * 128 : (m + 1) * 128]


def far_kernel(parts, after1, after2, out):
    total = sum8(parts)
    for m in range(8):
        out[m] = total


def pass_kernel(share, after, out):
    out[...] = share[...]


ORDER = (0, 3, 2, 1)


def weight_kernel(j_ref, second_ref, first_ref, out, ordered):
    j = j_ref[0]
    for place, d in enumerate(ORDER):
        quarter = j ^ d
        at = pl.ds(pl.multiple_of((quarter & 1) * 128, 128), 128)
        rows = jnp.where(quarter < 2, second_ref[at, :], first_ref[at, :])
        ordered[place * 128 : (place + 1) * 128, :] = rows
    out[0], out[1] = split(ordered[...].T)


def natural(parts):
    return jnp.concatenate(
        [jnp.concatenate([part[t * 128 : (t + 1) * 128, :] for t in range(8)], axis=1) for part in parts], axis=0
    )


def middle_kernel(block, w_ref, own, got, out):
    proj = split(natural((own, got)))
    for t in range(2):
        rows = slice(t * 256, (t + 1) * 256)
        out[rows] = block[rows] - mul3((w_ref[0, rows, :256], w_ref[1, rows, :256]), proj)


def update_kernel(middle, w_ref, got, last, out_ref, out, sems):
    proj = split(natural((got, last)))
    stores = []
    for t in range(4):
        rows = slice(t * 128, (t + 1) * 128)
        out[rows] = middle[rows] - mul3((w_ref[0, rows, 256:], w_ref[1, rows, 256:]), proj)
        stores.append(pltpu.make_async_copy(out.at[rows], out_ref.at[rows], sems.at[t]))
        stores[t].start()
    for store in stores:
        store.wait()


def call(kernel, outs, args, scratch=(), scalars=0, inputs=None, out_spec=VMEM):
    single = not isinstance(outs, list)
    return pl.pallas_call(
        kernel,
        out_shape=outs,
        in_specs=inputs or [SMEM] * scalars + [VMEM] * (len(args) - scalars),
        out_specs=out_spec if single else [out_spec] * len(outs),
        scratch_shapes=list(scratch),
        compiler_params=PARAMS,
    )(*args)


def shape(*dims, dtype=F32):
    return jax.ShapeDtypeStruct(dims, dtype)


def exact(left, right):
    dims = (((0,), (0,)), ((), ()))
    return lax.dot_general(left, right, dims, precision=lax.Precision.HIGHEST, preferred_element_type=F32)


def trade(pieces, groups):
    return lax.all_to_all(pieces, ROW + COL, 0, 0, axis_index_groups=groups)


def fetch(value, d):
    def partner(i, n, core):
        return (i + 1) % n if i % 2 == core else (i - 1) % n

    pairs = [
        (device(x, y, z, c), device(partner(x, NX, c) if d & 2 else x, partner(y, NY, c) if d & 1 else y, z, c))
        for x in range(NX)
        for y in range(NY)
        for z in range(NZ)
        for c in range(2)
    ]
    return lax.ppermute(value, ROW + COL, pairs)


def local(vectors, reflectors_first, reflectors_second, factor_first, factor_second):
    core = lax.axis_index("core")
    scalar = core.astype(jnp.int32).reshape(1)
    j = label_x(lax.axis_index("x"), core) * 2 + label_y(lax.axis_index("y"), core)
    j = j.astype(jnp.int32).reshape(1)
    shards = jnp.concatenate([reflectors_second, reflectors_first], axis=0)
    mine = lax.all_to_all(jnp.broadcast_to(shards[None], (NZ,) + shards.shape), "z", 0, 0)
    other = lax.ppermute(mine, "core", [(0, 1), (1, 0)])
    block = call(split_kernel, [shape(512, 1024, dtype=BF16)] * 2, (vectors,))
    wide = shape(512, 512, dtype=BF16)
    diagonal, cross, *panels = call(
        diagonal_kernel,
        [shape(1024, 128), shape(8, 32, 128), wide, wide],
        (scalar, j, mine, other, reflectors_first, *block),
        (pltpu.VMEM((2, 8, 32, 512), F32),),
        scalars=2,
    )
    along_x, along_y = call(beside_kernel, [shape(1024, 128)] * 2, (j, *panels, *block), scalars=1)
    half = call(own_kernel, shape(1024, 128), (j, fetch(diagonal, 3), *panels, *block), scalars=1)
    by_core = jnp.stack([jnp.where(core == 0, mine, other), jnp.where(core == 0, other, mine)], axis=1)
    second = by_core[:, :, :16].reshape(256, 512)
    first = by_core[:, :, 16:].reshape(256, 512)
    w_first = exact(factor_first, first)
    cross = call(cross_kernel, shape(16, 256), (trade(cross, PARITY),))
    parts = (half, fetch(along_y, 1), fetch(along_x, 2), cross)
    parts = call(near_kernel, shape(8, 128, 128), parts, inputs=[VMEM, VMEM, VMEM, HBM])
    cross = lax.all_gather(cross, COL, axis=0, tiled=True)
    share = call(far_kernel, shape(8, 128, 128), (trade(parts, FAR), w_first, cross), inputs=[VMEM, HBM, HBM])
    share = trade(share, FAR).reshape(1024, 128)
    cross = call(cross_sum_kernel, shape(256, 256), (cross, *(fetch(cross, d) for d in (1, 2, 3))))
    share = call(pass_kernel, shape(1024, 128), (share, cross), inputs=[VMEM, HBM])
    got = {d: fetch(share, d) for d in (3, 2, 1)}
    w_second = exact(factor_second, second - exact(cross, w_first))
    weights = call(
        weight_kernel,
        shape(2, 512, 512, dtype=BF16),
        (j, w_second, w_first),
        (pltpu.VMEM((512, 512), F32),),
        scalars=1,
    )
    middle = call(middle_kernel, shape(512, 1024), (vectors, weights, share, got[3]))
    return call(
        update_kernel,
        shape(512, 1024),
        (middle, weights, got[2], got[1]),
        (pltpu.VMEM((512, 1024), F32), pltpu.SemaphoreType.DMA((4,))),
        out_spec=HBM,
    )


def solution(mesh):
    fine = Mesh(mesh.devices.reshape(NX, NY, NZ, 2), ROW + COL)
    return jax.shard_map(
        local,
        mesh=fine,
        in_specs=(P(ROW, COL), P(COL, ROW), P(COL, ROW), P(), P()),
        out_specs=P(ROW, COL),
        check_vma=False,
    )
```

```python
import jax
import jax.numpy as jnp
from jax import lax
from jax.experimental import pallas as pl
from jax.experimental.pallas import tpu as pltpu
from jax.sharding import Mesh, PartitionSpec as P

ROW = ("x", "y")
COL = ("z", "core")
NX, NY, NZ = 4, 8, 8
F32, BF16 = jnp.float32, jnp.bfloat16
VMEM = pl.BlockSpec(memory_space=pltpu.VMEM)
SMEM = pl.BlockSpec(memory_space=pltpu.SMEM)
HBM = pl.BlockSpec(memory_space=pltpu.HBM)
PARAMS = pltpu.CompilerParams(vmem_limit_bytes=48 * 2**20)


def device(x, y, z, core):
    return ((x % NX * NY + y % NY) * NZ + z) * 2 + core


def label_x(x, core):
    return (x >> 1) ^ (x & 1 & ~core)


def label_y(y, core):
    y = (y - core) & 7
    return (y & 1) ^ (y >> 2)


FAR = [
    [
        device(x, y, z, core)
        for x in range(NX)
        for y in range(NY)
        if (label_x(x, core), label_y(y, core)) == (px, py)
    ]
    for z in range(NZ)
    for core in range(2)
    for px in range(2)
    for py in range(2)
]


def split(value):
    high = value.astype(BF16)
    return high, (value - high.astype(F32)).astype(BF16)


def mul(a, b):
    return jnp.dot(a, b, preferred_element_type=F32)


def mul_nt(a, b):
    return lax.dot_general(a, b, (((1,), (1,)), ((), ())), preferred_element_type=F32)


def mul3(a, b, mul=mul):
    return mul(a[0], b[0]) + (mul(a[0], b[1]) + mul(a[1], b[0]))


def split_kernel(block_ref, high, low):
    high[...], low[...] = split(block_ref[...])


def quarter(j, d, high, low, cross, block_high, block_low, out):
    at = pl.ds(pl.multiple_of((j ^ d) * 128, 128), 128)
    rows = high[at, :], low[at, :]
    for t in range(4):
        at = slice(t * 256, (t + 1) * 256)
        value = mul3(rows, (block_high[:, at], block_low[:, at]))
        for half in range(2):
            to = (2 * t + half) * 128
            out[to : to + 128, :] = value[:, half * 128 : (half + 1) * 128]
    at = pl.ds(pl.multiple_of((j ^ d) * 64, 64), 64)
    out[1024:1088, :] = cross[at, :128]
    out[1088:, :] = cross[at, 128:]


def diagonal_kernel(core_ref, j_ref, mine_ref, other_ref, block_high, block_low, out, cross, high, low, both):
    core = core_ref[0]
    both[0] = mine_ref[...]
    both[1] = other_ref[...]
    for c in range(2):
        from_core = both.at[core ^ c]
        for z in range(8):
            for panel in range(2):
                h, l = split(from_core[z, panel * 16 : panel * 16 + 16, :])
                at = (z // 2) * 128 + panel * 64 + (z % 2) * 32 + c * 16
                high[at : at + 16, :] = h
                low[at : at + 16, :] = l

    def whole(panel, ref):
        return jnp.concatenate([ref[q * 128 + panel * 64 : q * 128 + panel * 64 + 64, :] for q in range(4)], axis=0)

    cross[...] = mul3((whole(1, high), whole(1, low)), (whole(0, high), whole(0, low)), mul_nt)
    quarter(j_ref[0], 3, high, low, cross, block_high, block_low, out)


def beside_kernel(j_ref, cross, high, low, block_high, block_low, *outs):
    for d, out in zip((2, 1), outs):
        quarter(j_ref[0], d, high, low, cross, block_high, block_low, out)


def own_kernel(j_ref, got, cross, high, low, block_high, block_low, out):
    quarter(j_ref[0], 0, high, low, cross, block_high, block_low, out)
    out[...] += got[...]


def near_kernel(half, got1, got2, out):
    total = half[...] + (got1[...] + got2[...])
    for m in range(8):
        out[m, :128, :] = total[m * 128 : (m + 1) * 128]
        out[m, 128:, :] = total[1024 + m * 16 : 1040 + m * 16]


def far_kernel(parts, after, out):
    total = ((parts[0] + parts[1]) + (parts[2] + parts[3])) + ((parts[4] + parts[5]) + (parts[6] + parts[7]))
    for m in range(8):
        out[m] = total


def share_kernel(parts, out):
    for m in range(8):
        out[m * 128 : (m + 1) * 128, :] = parts[m, :128]
        out[1024 + m * 16 : 1040 + m * 16, :] = parts[m, 128:]


ORDER = (0, 3, 2, 1)


def prepare_kernel(j_ref, second_ref, w_ref, factor_ref, panel, weights, factor, turned):
    panel[...] = second_ref[...].T
    turned[...] = factor_ref[...].T
    at = [pl.ds(pl.multiple_of((j_ref[0] ^ d) * 64, 64), 64) for d in ORDER]
    weights[0], weights[1] = split(jnp.concatenate([w_ref[rows, :] for rows in at], axis=0).T)
    factor[0], factor[1] = split(jnp.concatenate([turned[rows, :] for rows in at], axis=0).T)


def natural(part):
    return jnp.concatenate([part[t * 128 : (t + 1) * 128, :] for t in range(8)], axis=1)


def cross_of(part):
    return jnp.concatenate([part[1024:1088, :], part[1088:, :]], axis=1)


def middle_kernel(block, weights, own, got, out):
    proj = split(jnp.concatenate([natural(own)[64:], natural(got)[64:]], axis=0))
    for t in range(2):
        rows = slice(t * 256, (t + 1) * 256)
        out[rows] = block[rows] - mul3((weights[0, rows, :128], weights[1, rows, :128]), proj)


def update_kernel(middle, panel, weights, factor, own, got3, got2, got1, out_ref, out, sems):
    parts = (own, got3, got2, got1)
    cross = split(jnp.concatenate([cross_of(part) for part in parts], axis=0))
    rest = panel[...] - mul3((weights[0], weights[1]), cross)
    second = split(mul3(split(rest), (factor[0], factor[1])))
    quarters = [natural(part) for part in parts]
    left = [jnp.concatenate([second[i], weights[i, :, 128:]], axis=1) for i in range(2)]
    rows = [quarter[:64] for quarter in quarters] + [quarter[64:] for quarter in quarters[2:]]
    right = split(jnp.concatenate(rows, axis=0))
    stores = []
    for t in range(4):
        at = slice(t * 128, (t + 1) * 128)
        out[at] = middle[at] - mul3((left[0][at], left[1][at]), right)
        stores.append(pltpu.make_async_copy(out.at[at], out_ref.at[at], sems.at[t]))
        stores[t].start()
    for store in stores:
        store.wait()


def call(kernel, outs, args, scratch=(), scalars=0, inputs=None, out_spec=VMEM):
    single = not isinstance(outs, list)
    return pl.pallas_call(
        kernel,
        out_shape=outs,
        in_specs=inputs or [SMEM] * scalars + [VMEM] * (len(args) - scalars),
        out_specs=out_spec if single else [out_spec] * len(outs),
        scratch_shapes=list(scratch),
        compiler_params=PARAMS,
    )(*args)


def shape(*dims, dtype=F32):
    return jax.ShapeDtypeStruct(dims, dtype)


def exact(left, right):
    dims = (((0,), (0,)), ((), ()))
    return lax.dot_general(left, right, dims, precision=lax.Precision.HIGHEST, preferred_element_type=F32)


def trade(pieces):
    return lax.all_to_all(pieces, ROW + COL, 0, 0, axis_index_groups=FAR)


def fetch(value, d):
    def partner(i, n, core):
        return (i + 1) % n if i % 2 == core else (i - 1) % n

    pairs = [
        (device(x, y, z, c), device(partner(x, NX, c) if d & 2 else x, partner(y, NY, c) if d & 1 else y, z, c))
        for x in range(NX)
        for y in range(NY)
        for z in range(NZ)
        for c in range(2)
    ]
    return lax.ppermute(value, ROW + COL, pairs)


def local(vectors, reflectors_first, reflectors_second, factor_first, factor_second):
    core = lax.axis_index("core")
    scalar = core.astype(jnp.int32).reshape(1)
    j = label_x(lax.axis_index("x"), core) * 2 + label_y(lax.axis_index("y"), core)
    j = j.astype(jnp.int32).reshape(1)
    shards = jnp.concatenate([reflectors_second, reflectors_first], axis=0)
    mine = lax.all_to_all(jnp.broadcast_to(shards[None], (NZ,) + shards.shape), "z", 0, 0)
    other = lax.ppermute(mine, "core", [(0, 1), (1, 0)])
    block = call(split_kernel, [shape(512, 1024, dtype=BF16)] * 2, (vectors,))
    wide = shape(512, 512, dtype=BF16)
    diagonal, *panels = call(
        diagonal_kernel,
        [shape(1152, 128), shape(256, 256), wide, wide],
        (scalar, j, mine, other, *block),
        (pltpu.VMEM((2, 8, 32, 512), F32),),
        scalars=2,
    )
    along_x, along_y = call(beside_kernel, [shape(1152, 128)] * 2, (j, *panels, *block), scalars=1)
    half = call(own_kernel, shape(1152, 128), (j, fetch(diagonal, 3), *panels, *block), scalars=1)
    by_core = jnp.stack([jnp.where(core == 0, mine, other), jnp.where(core == 0, other, mine)], axis=1)
    second = by_core[:, :, :16].reshape(256, 512)
    first = by_core[:, :, 16:].reshape(256, 512)
    w_first = exact(factor_first, first)
    parts = call(near_kernel, shape(8, 144, 128), (half, fetch(along_y, 1), fetch(along_x, 2)))
    parts = call(far_kernel, shape(8, 144, 128), (trade(parts), w_first), inputs=[VMEM, HBM])
    share = call(share_kernel, shape(1152, 128), (trade(parts),))
    got = {d: fetch(share, d) for d in (3, 2, 1)}
    panel, weights, factor = call(
        prepare_kernel,
        [shape(512, 256), shape(2, 512, 256, dtype=BF16), shape(2, 256, 256, dtype=BF16)],
        (j, second, w_first, factor_second),
        (pltpu.VMEM((256, 256), F32),),
        scalars=1,
    )
    middle = call(middle_kernel, shape(512, 1024), (vectors, weights, share, got[3]))
    return call(
        update_kernel,
        shape(512, 1024),
        (middle, panel, weights, factor, share, got[3], got[2], got[1]),
        (pltpu.VMEM((512, 1024), F32), pltpu.SemaphoreType.DMA((4,))),
        out_spec=HBM,
    )


def solution(mesh):
    fine = Mesh(mesh.devices.reshape(NX, NY, NZ, 2), ROW + COL)
    return jax.shard_map(
        local,
        mesh=fine,
        in_specs=(P(ROW, COL), P(COL, ROW), P(COL, ROW), P(), P()),
        out_specs=P(ROW, COL),
        check_vma=False,
    )
```

```python
import jax
import jax.numpy as jnp
from jax import lax
from jax.experimental import pallas as pl
from jax.experimental.pallas import tpu as pltpu
from jax.sharding import Mesh, PartitionSpec as P

ROW = ("x", "y")
COL = ("z", "core")
NX, NY, NZ = 4, 8, 8
F32, BF16 = jnp.float32, jnp.bfloat16
VMEM = pl.BlockSpec(memory_space=pltpu.VMEM)
SMEM = pl.BlockSpec(memory_space=pltpu.SMEM)
HBM = pl.BlockSpec(memory_space=pltpu.HBM)
PARAMS = pltpu.CompilerParams(vmem_limit_bytes=48 * 2**20)


def device(x, y, z, core):
    return ((x % NX * NY + y % NY) * NZ + z) * 2 + core


def label_x(x, core):
    return (x >> 1) ^ (x & 1 & ~core)


def label_y(y, core):
    y = (y - core) & 7
    return (y & 1) ^ (y >> 2)


FAR = [
    [
        device(x, y, z, core)
        for x in range(NX)
        for y in range(NY)
        if (label_x(x, core), label_y(y, core)) == (px, py)
    ]
    for z in range(NZ)
    for core in range(2)
    for px in range(2)
    for py in range(2)
]


def split(value):
    high = value.astype(BF16)
    return high, (value - high.astype(F32)).astype(BF16)


def mul(a, b):
    return jnp.dot(a, b, preferred_element_type=F32)


def mul_nt(a, b):
    return lax.dot_general(a, b, (((1,), (1,)), ((), ())), preferred_element_type=F32)


def mul3(a, b, mul=mul):
    return mul(a[0], b[0]) + (mul(a[0], b[1]) + mul(a[1], b[0]))


def split_kernel(block_ref, high, low):
    high[...], low[...] = split(block_ref[...])


def quarter(j, d, high, low, cross, block_high, block_low, out):
    at = pl.ds(pl.multiple_of((j ^ d) * 128, 128), 128)
    rows = high[at, :], low[at, :]
    for t in range(4):
        at = slice(t * 256, (t + 1) * 256)
        value = mul3(rows, (block_high[:, at], block_low[:, at]))
        for half in range(2):
            to = (2 * t + half) * 128
            out[to : to + 128, :] = value[:, half * 128 : (half + 1) * 128]
    at = pl.ds(pl.multiple_of((j ^ d) * 64, 64), 64)
    out[1024:1088, :] = cross[at, :128]
    out[1088:, :] = cross[at, 128:]


def diagonal_kernel(core_ref, j_ref, mine_ref, other_ref, block_high, block_low, out, cross, high, low, both):
    core = core_ref[0]
    both[0] = mine_ref[...]
    both[1] = other_ref[...]
    for c in range(2):
        from_core = both.at[core ^ c]
        for z in range(8):
            for panel in range(2):
                h, l = split(from_core[z, panel * 16 : panel * 16 + 16, :])
                at = (z // 2) * 128 + panel * 64 + (z % 2) * 32 + c * 16
                high[at : at + 16, :] = h
                low[at : at + 16, :] = l

    def whole(panel, ref):
        return jnp.concatenate([ref[q * 128 + panel * 64 : q * 128 + panel * 64 + 64, :] for q in range(4)], axis=0)

    cross[...] = mul3((whole(1, high), whole(1, low)), (whole(0, high), whole(0, low)), mul_nt)
    quarter(j_ref[0], 3, high, low, cross, block_high, block_low, out)


def beside_kernel(j_ref, cross, high, low, block_high, block_low, *outs):
    for d, out in zip((2, 1), outs):
        quarter(j_ref[0], d, high, low, cross, block_high, block_low, out)


def own_kernel(j_ref, got, cross, high, low, block_high, block_low, out):
    quarter(j_ref[0], 0, high, low, cross, block_high, block_low, out)
    out[...] += got[...]


def near_kernel(half, got1, got2, out):
    total = half[...] + (got1[...] + got2[...])
    for m in range(8):
        out[m, :128, :] = total[m * 128 : (m + 1) * 128]
        out[m, 128:, :] = total[1024 + m * 16 : 1040 + m * 16]


def far_kernel(parts, out):
    total = ((parts[0] + parts[1]) + (parts[2] + parts[3])) + ((parts[4] + parts[5]) + (parts[6] + parts[7]))
    for m in range(8):
        out[m] = total


def share_kernel(parts, out):
    for m in range(8):
        out[m * 128 : (m + 1) * 128, :] = parts[m, :128]
        out[1024 + m * 16 : 1040 + m * 16, :] = parts[m, 128:]


ORDER = (0, 3, 2, 1)


def prepare_kernel(j_ref, second_ref, first_ref, second_factor, first_factor, panel, weights, factor, turned):
    at = [pl.ds(pl.multiple_of((j_ref[0] ^ d) * 64, 64), 64) for d in ORDER]

    def ordered(ref):
        turned[...] = ref[...].T
        return split(jnp.concatenate([turned[rows, :] for rows in at], axis=0).T)

    panel[...] = second_ref[...].T
    weights[0], weights[1] = split(mul3(split(first_ref[...].T), ordered(first_factor)))
    factor[0], factor[1] = ordered(second_factor)


def natural(part):
    return jnp.concatenate([part[t * 128 : (t + 1) * 128, :] for t in range(8)], axis=1)


def cross_of(part):
    return jnp.concatenate([part[1024:1088, :], part[1088:, :]], axis=1)


def middle_kernel(block, weights, own, got, out):
    proj = split(jnp.concatenate([natural(own)[64:], natural(got)[64:]], axis=0))
    for t in range(2):
        rows = slice(t * 256, (t + 1) * 256)
        out[rows] = block[rows] - mul3((weights[0, rows, :128], weights[1, rows, :128]), proj)


def update_kernel(middle, panel, weights, factor, own, got3, got2, got1, out_ref, out, sems):
    parts = (own, got3, got2, got1)
    cross = split(jnp.concatenate([cross_of(part) for part in parts], axis=0))
    rest = panel[...] - mul3((weights[0], weights[1]), cross)
    second = split(mul3(split(rest), (factor[0], factor[1])))
    quarters = [natural(part) for part in parts]
    left = [jnp.concatenate([second[i], weights[i, :, 128:]], axis=1) for i in range(2)]
    rows = [quarter[:64] for quarter in quarters] + [quarter[64:] for quarter in quarters[2:]]
    right = split(jnp.concatenate(rows, axis=0))
    stores = []
    for t in range(4):
        at = slice(t * 128, (t + 1) * 128)
        out[at] = middle[at] - mul3((left[0][at], left[1][at]), right)
        stores.append(pltpu.make_async_copy(out.at[at], out_ref.at[at], sems.at[t]))
        stores[t].start()
    for store in stores:
        store.wait()


def call(kernel, outs, args, scratch=(), scalars=0, inputs=None, out_spec=VMEM):
    single = not isinstance(outs, list)
    return pl.pallas_call(
        kernel,
        out_shape=outs,
        in_specs=inputs or [SMEM] * scalars + [VMEM] * (len(args) - scalars),
        out_specs=out_spec if single else [out_spec] * len(outs),
        scratch_shapes=list(scratch),
        compiler_params=PARAMS,
    )(*args)


def shape(*dims, dtype=F32):
    return jax.ShapeDtypeStruct(dims, dtype)


def trade(pieces):
    return lax.all_to_all(pieces, ROW + COL, 0, 0, axis_index_groups=FAR)


def fetch(value, d):
    def partner(i, n, core):
        return (i + 1) % n if i % 2 == core else (i - 1) % n

    pairs = [
        (device(x, y, z, c), device(partner(x, NX, c) if d & 2 else x, partner(y, NY, c) if d & 1 else y, z, c))
        for x in range(NX)
        for y in range(NY)
        for z in range(NZ)
        for c in range(2)
    ]
    return lax.ppermute(value, ROW + COL, pairs)


def local(vectors, reflectors_first, reflectors_second, factor_first, factor_second):
    core = lax.axis_index("core")
    scalar = core.astype(jnp.int32).reshape(1)
    j = label_x(lax.axis_index("x"), core) * 2 + label_y(lax.axis_index("y"), core)
    j = j.astype(jnp.int32).reshape(1)
    shards = jnp.concatenate([reflectors_second, reflectors_first], axis=0)
    mine = lax.all_to_all(jnp.broadcast_to(shards[None], (NZ,) + shards.shape), "z", 0, 0)
    other = lax.ppermute(mine, "core", [(0, 1), (1, 0)])
    block = call(split_kernel, [shape(512, 1024, dtype=BF16)] * 2, (vectors,))
    wide = shape(512, 512, dtype=BF16)
    diagonal, *panels = call(
        diagonal_kernel,
        [shape(1152, 128), shape(256, 256), wide, wide],
        (scalar, j, mine, other, *block),
        (pltpu.VMEM((2, 8, 32, 512), F32),),
        scalars=2,
    )
    along_x, along_y = call(beside_kernel, [shape(1152, 128)] * 2, (j, *panels, *block), scalars=1)
    half = call(own_kernel, shape(1152, 128), (j, fetch(diagonal, 3), *panels, *block), scalars=1)
    by_core = jnp.stack([jnp.where(core == 0, mine, other), jnp.where(core == 0, other, mine)], axis=1)
    second = by_core[:, :, :16].reshape(256, 512)
    first = by_core[:, :, 16:].reshape(256, 512)
    parts = call(near_kernel, shape(8, 144, 128), (half, fetch(along_y, 1), fetch(along_x, 2)))
    parts = call(far_kernel, shape(8, 144, 128), (trade(parts),))
    share = call(share_kernel, shape(1152, 128), (trade(parts),))
    got = {d: fetch(share, d) for d in (3, 2, 1)}
    panel, weights, factor = call(
        prepare_kernel,
        [shape(512, 256), shape(2, 512, 256, dtype=BF16), shape(2, 256, 256, dtype=BF16)],
        (j, second, first, factor_second, factor_first),
        (pltpu.VMEM((256, 256), F32),),
        scalars=1,
    )
    middle = call(middle_kernel, shape(512, 1024), (vectors, weights, share, got[3]))
    return call(
        update_kernel,
        shape(512, 1024),
        (middle, panel, weights, factor, share, got[3], got[2], got[1]),
        (pltpu.VMEM((512, 1024), F32), pltpu.SemaphoreType.DMA((4,))),
        out_spec=HBM,
    )


def solution(mesh):
    fine = Mesh(mesh.devices.reshape(NX, NY, NZ, 2), ROW + COL)
    return jax.shard_map(
        local,
        mesh=fine,
        in_specs=(P(ROW, COL), P(COL, ROW), P(COL, ROW), P(), P()),
        out_specs=P(ROW, COL),
        check_vma=False,
    )
```

```python
import jax
import jax.numpy as jnp
from jax import lax
from jax.experimental import pallas as pl
from jax.experimental.pallas import tpu as pltpu
from jax.sharding import Mesh, PartitionSpec as P

ROW = ("x", "y")
COL = ("z", "core")
NX, NY, NZ = 4, 8, 8
F32, BF16 = jnp.float32, jnp.bfloat16
VMEM = pl.BlockSpec(memory_space=pltpu.VMEM)
SMEM = pl.BlockSpec(memory_space=pltpu.SMEM)
HBM = pl.BlockSpec(memory_space=pltpu.HBM)
PARAMS = pltpu.CompilerParams(vmem_limit_bytes=48 * 2**20)


def device(x, y, z, core):
    return ((x % NX * NY + y % NY) * NZ + z) * 2 + core


def label_x(x, core):
    return (x >> 1) ^ (x & 1 & ~core)


def label_y(y, core):
    y = (y - core) & 7
    return (y & 1) ^ (y >> 2)


FAR = [
    [
        device(x, y, z, core)
        for x in range(NX)
        for y in range(NY)
        if (label_x(x, core), label_y(y, core)) == (px, py)
    ]
    for z in range(NZ)
    for core in range(2)
    for px in range(2)
    for py in range(2)
]


def split(value):
    high = value.astype(BF16)
    return high, (value - high.astype(F32)).astype(BF16)


def mul(a, b):
    return jnp.dot(a, b, preferred_element_type=F32)


def mul_nt(a, b):
    return lax.dot_general(a, b, (((1,), (1,)), ((), ())), preferred_element_type=F32)


def mul3(a, b, mul=mul):
    return mul(a[0], b[0]) + (mul(a[0], b[1]) + mul(a[1], b[0]))


def split_kernel(block_ref, high, low):
    high[...], low[...] = split(block_ref[...])


def quarter(j, d, high, low, cross, block_high, block_low, out):
    at = pl.ds(pl.multiple_of((j ^ d) * 128, 128), 128)
    rows = high[at, :], low[at, :]
    for t in range(4):
        at = slice(t * 256, (t + 1) * 256)
        value = mul3(rows, (block_high[:, at], block_low[:, at]))
        for half in range(2):
            to = (2 * t + half) * 128
            out[to : to + 128, :] = value[:, half * 128 : (half + 1) * 128]
    at = pl.ds(pl.multiple_of((j ^ d) * 64, 64), 64)
    out[1024:1088, :] = cross[at, :128]
    out[1088:, :] = cross[at, 128:]


def diagonal_kernel(core_ref, j_ref, mine_ref, other_ref, block_high, block_low, out, cross, high, low, both):
    core = core_ref[0]
    both[0] = mine_ref[...]
    both[1] = other_ref[...]
    for c in range(2):
        from_core = both.at[core ^ c]
        for z in range(8):
            for panel in range(2):
                h, l = split(from_core[z, panel * 16 : panel * 16 + 16, :])
                at = (z // 2) * 128 + panel * 64 + (z % 2) * 32 + c * 16
                high[at : at + 16, :] = h
                low[at : at + 16, :] = l

    def whole(panel, ref):
        return jnp.concatenate([ref[q * 128 + panel * 64 : q * 128 + panel * 64 + 64, :] for q in range(4)], axis=0)

    cross[...] = mul3((whole(1, high), whole(1, low)), (whole(0, high), whole(0, low)), mul_nt)
    quarter(j_ref[0], 3, high, low, cross, block_high, block_low, out)


def beside_kernel(j_ref, cross, high, low, block_high, block_low, *outs):
    for d, out in zip((2, 1), outs):
        quarter(j_ref[0], d, high, low, cross, block_high, block_low, out)


def own_kernel(j_ref, got, cross, high, low, block_high, block_low, out):
    quarter(j_ref[0], 0, high, low, cross, block_high, block_low, out)
    out[...] += got[...]


def near_kernel(half, got1, got2, out):
    total = half[...] + (got1[...] + got2[...])
    for m in range(8):
        out[m, :128, :] = total[m * 128 : (m + 1) * 128]
        out[m, 128:, :] = total[1024 + m * 16 : 1040 + m * 16]


def far_kernel(parts, out):
    total = ((parts[0] + parts[1]) + (parts[2] + parts[3])) + ((parts[4] + parts[5]) + (parts[6] + parts[7]))
    for m in range(8):
        out[m] = total


def share_kernel(parts, out):
    for m in range(8):
        out[m * 128 : (m + 1) * 128, :] = parts[m, :128]
        out[1024 + m * 16 : 1040 + m * 16, :] = parts[m, 128:]


ORDER = (0, 3, 2, 1)


def prepare_kernel(
    core_ref, j_ref, mine_ref, other_ref, second_factor, first_factor, panel, weights, factor, turned, both, panels
):
    both[0] = mine_ref[...]
    both[1] = other_ref[...]
    for c in range(2):
        from_core = both.at[core_ref[0] ^ c]
        for z in range(8):
            to = slice(z * 32 + c * 16, z * 32 + c * 16 + 16)
            panels[0, to, :] = from_core[z, :16, :]
            panels[1, to, :] = from_core[z, 16:, :]
    at = [pl.ds(pl.multiple_of((j_ref[0] ^ d) * 64, 64), 64) for d in ORDER]

    def ordered(ref):
        turned[...] = ref[...].T
        return split(jnp.concatenate([turned[rows, :] for rows in at], axis=0).T)

    panel[...] = panels[0].T
    weights[0], weights[1] = split(mul3(split(panels[1].T), ordered(first_factor)))
    factor[0], factor[1] = ordered(second_factor)


def natural(part):
    return jnp.concatenate([part[t * 128 : (t + 1) * 128, :] for t in range(8)], axis=1)


def cross_of(part):
    return jnp.concatenate([part[1024:1088, :], part[1088:, :]], axis=1)


def middle_kernel(block, weights, own, got, out):
    proj = split(jnp.concatenate([natural(own)[64:], natural(got)[64:]], axis=0))
    for t in range(2):
        rows = slice(t * 256, (t + 1) * 256)
        out[rows] = block[rows] - mul3((weights[0, rows, :128], weights[1, rows, :128]), proj)


def update_kernel(middle, panel, weights, factor, own, got3, got2, got1, out_ref, out, sems):
    parts = (own, got3, got2, got1)
    cross = split(jnp.concatenate([cross_of(part) for part in parts], axis=0))
    rest = panel[...] - mul3((weights[0], weights[1]), cross)
    second = split(mul3(split(rest), (factor[0], factor[1])))
    quarters = [natural(part) for part in parts]
    left = [jnp.concatenate([second[i], weights[i, :, 128:]], axis=1) for i in range(2)]
    rows = [quarter[:64] for quarter in quarters] + [quarter[64:] for quarter in quarters[2:]]
    right = split(jnp.concatenate(rows, axis=0))
    stores = []
    for t in range(4):
        at = slice(t * 128, (t + 1) * 128)
        out[at] = middle[at] - mul3((left[0][at], left[1][at]), right)
        stores.append(pltpu.make_async_copy(out.at[at], out_ref.at[at], sems.at[t]))
        stores[t].start()
    for store in stores:
        store.wait()


def call(kernel, outs, args, scratch=(), scalars=0, inputs=None, out_spec=VMEM):
    single = not isinstance(outs, list)
    return pl.pallas_call(
        kernel,
        out_shape=outs,
        in_specs=inputs or [SMEM] * scalars + [VMEM] * (len(args) - scalars),
        out_specs=out_spec if single else [out_spec] * len(outs),
        scratch_shapes=list(scratch),
        compiler_params=PARAMS,
    )(*args)


def shape(*dims, dtype=F32):
    return jax.ShapeDtypeStruct(dims, dtype)


def trade(pieces):
    return lax.all_to_all(pieces, ROW + COL, 0, 0, axis_index_groups=FAR)


def fetch(value, d):
    def partner(i, n, core):
        return (i + 1) % n if i % 2 == core else (i - 1) % n

    pairs = [
        (device(x, y, z, c), device(partner(x, NX, c) if d & 2 else x, partner(y, NY, c) if d & 1 else y, z, c))
        for x in range(NX)
        for y in range(NY)
        for z in range(NZ)
        for c in range(2)
    ]
    return lax.ppermute(value, ROW + COL, pairs)


def local(vectors, reflectors_first, reflectors_second, factor_first, factor_second):
    core = lax.axis_index("core")
    scalar = core.astype(jnp.int32).reshape(1)
    j = label_x(lax.axis_index("x"), core) * 2 + label_y(lax.axis_index("y"), core)
    j = j.astype(jnp.int32).reshape(1)
    shards = jnp.concatenate([reflectors_second, reflectors_first], axis=0)
    mine = lax.all_to_all(jnp.broadcast_to(shards[None], (NZ,) + shards.shape), "z", 0, 0)
    other = lax.ppermute(mine, "core", [(0, 1), (1, 0)])
    block = call(split_kernel, [shape(512, 1024, dtype=BF16)] * 2, (vectors,))
    wide = shape(512, 512, dtype=BF16)
    diagonal, *panels = call(
        diagonal_kernel,
        [shape(1152, 128), shape(256, 256), wide, wide],
        (scalar, j, mine, other, *block),
        (pltpu.VMEM((2, 8, 32, 512), F32),),
        scalars=2,
    )
    along_x, along_y = call(beside_kernel, [shape(1152, 128)] * 2, (j, *panels, *block), scalars=1)
    half = call(own_kernel, shape(1152, 128), (j, fetch(diagonal, 3), *panels, *block), scalars=1)
    parts = call(near_kernel, shape(8, 144, 128), (half, fetch(along_y, 1), fetch(along_x, 2)))
    parts = call(far_kernel, shape(8, 144, 128), (trade(parts),))
    share = call(share_kernel, shape(1152, 128), (trade(parts),))
    got = {d: fetch(share, d) for d in (3, 2, 1)}
    panel, weights, factor = call(
        prepare_kernel,
        [shape(512, 256), shape(2, 512, 256, dtype=BF16), shape(2, 256, 256, dtype=BF16)],
        (scalar, j, mine, other, factor_second, factor_first),
        (pltpu.VMEM((256, 256), F32), pltpu.VMEM((2, 8, 32, 512), F32), pltpu.VMEM((2, 256, 512), F32)),
        scalars=2,
    )
    middle = call(middle_kernel, shape(512, 1024), (vectors, weights, share, got[3]))
    return call(
        update_kernel,
        shape(512, 1024),
        (middle, panel, weights, factor, share, got[3], got[2], got[1]),
        (pltpu.VMEM((512, 1024), F32), pltpu.SemaphoreType.DMA((4,))),
        out_spec=HBM,
    )


def solution(mesh):
    fine = Mesh(mesh.devices.reshape(NX, NY, NZ, 2), ROW + COL)
    return jax.shard_map(
        local,
        mesh=fine,
        in_specs=(P(ROW, COL), P(COL, ROW), P(COL, ROW), P(), P()),
        out_specs=P(ROW, COL),
        check_vma=False,
    )
```

```python
import jax
import jax.numpy as jnp
from jax import lax
from jax.experimental import pallas as pl
from jax.experimental.pallas import tpu as pltpu
from jax.sharding import Mesh, PartitionSpec as P

ROW = ("x", "y")
COL = ("z", "core")
NX, NY, NZ = 4, 8, 8
F32, BF16 = jnp.float32, jnp.bfloat16
VMEM = pl.BlockSpec(memory_space=pltpu.VMEM)
SMEM = pl.BlockSpec(memory_space=pltpu.SMEM)
HBM = pl.BlockSpec(memory_space=pltpu.HBM)
PARAMS = pltpu.CompilerParams(vmem_limit_bytes=28 * 2**20)


def device(x, y, z, core):
    return ((x % NX * NY + y % NY) * NZ + z) * 2 + core


def label_x(x, core):
    return (x >> 1) ^ (x & 1 & ~core)


def label_y(y, core):
    y = (y - core) & 7
    return (y & 1) ^ (y >> 2)


FAR = [
    [
        device(x, y, z, core)
        for x in range(NX)
        for y in range(NY)
        if (label_x(x, core), label_y(y, core)) == (px, py)
    ]
    for z in range(NZ)
    for core in range(2)
    for px in range(2)
    for py in range(2)
]


def split(value):
    high = value.astype(BF16)
    return high, (value - high.astype(F32)).astype(BF16)


def mul(a, b):
    return jnp.dot(a, b, preferred_element_type=F32)


def mul_nt(a, b):
    return lax.dot_general(a, b, (((1,), (1,)), ((), ())), preferred_element_type=F32)


def mul3(a, b, mul=mul):
    return mul(a[0], b[0]) + (mul(a[0], b[1]) + mul(a[1], b[0]))


def split_kernel(block_ref, high, low):
    high[...], low[...] = split(block_ref[...])


def quarter(j, d, high, low, cross, block_high, block_low, out):
    at = pl.ds(pl.multiple_of((j ^ d) * 128, 128), 128)
    rows = high[at, :], low[at, :]
    for t in range(4):
        at = slice(t * 256, (t + 1) * 256)
        value = mul3(rows, (block_high[:, at], block_low[:, at]))
        for half in range(2):
            to = (2 * t + half) * 128
            out[to : to + 128, :] = value[:, half * 128 : (half + 1) * 128]
    at = pl.ds(pl.multiple_of((j ^ d) * 64, 64), 64)
    out[1024:1088, :] = cross[at, :128]
    out[1088:, :] = cross[at, 128:]


def project_kernel(
    core_ref, j_ref, mine_ref, other_ref, block_high, block_low, out3, out2, out1, cross, high, low, both
):
    core = core_ref[0]
    both[0] = mine_ref[...]
    both[1] = other_ref[...]
    for c in range(2):
        from_core = both.at[core ^ c]
        for z in range(8):
            for panel in range(2):
                h, l = split(from_core[z, panel * 16 : panel * 16 + 16, :])
                at = (z // 2) * 128 + panel * 64 + (z % 2) * 32 + c * 16
                high[at : at + 16, :] = h
                low[at : at + 16, :] = l

    def whole(panel, ref):
        return jnp.concatenate([ref[q * 128 + panel * 64 : q * 128 + panel * 64 + 64, :] for q in range(4)], axis=0)

    cross[...] = mul3((whole(1, high), whole(1, low)), (whole(0, high), whole(0, low)), mul_nt)
    for d, out in ((3, out3), (2, out2), (1, out1)):
        quarter(j_ref[0], d, high, low, cross, block_high, block_low, out)


def own_kernel(j_ref, got, cross, high, low, block_high, block_low, out):
    quarter(j_ref[0], 0, high, low, cross, block_high, block_low, out)
    out[...] += got[...]


def near_kernel(half, got1, got2, out):
    total = half[...] + (got1[...] + got2[...])
    for m in range(8):
        out[m, :128, :] = total[m * 128 : (m + 1) * 128]
        out[m, 128:, :] = total[1024 + m * 16 : 1040 + m * 16]


def far_kernel(parts, out):
    total = ((parts[0] + parts[1]) + (parts[2] + parts[3])) + ((parts[4] + parts[5]) + (parts[6] + parts[7]))
    for m in range(8):
        out[m] = total


def share_kernel(parts, out):
    for m in range(8):
        out[m * 128 : (m + 1) * 128, :] = parts[m, :128]
        out[1024 + m * 16 : 1040 + m * 16, :] = parts[m, 128:]


ORDER = (0, 3, 2, 1)


def prepare_kernel(
    core_ref, j_ref, mine_ref, other_ref, second_factor, first_factor, panel, weights, factor, turned, both, panels
):
    both[0] = mine_ref[...]
    both[1] = other_ref[...]
    for c in range(2):
        from_core = both.at[core_ref[0] ^ c]
        for z in range(8):
            to = slice(z * 32 + c * 16, z * 32 + c * 16 + 16)
            panels[0, to, :] = from_core[z, :16, :]
            panels[1, to, :] = from_core[z, 16:, :]
    at = [pl.ds(pl.multiple_of((j_ref[0] ^ d) * 64, 64), 64) for d in ORDER]

    def ordered(ref):
        turned[...] = ref[...].T
        return split(jnp.concatenate([turned[rows, :] for rows in at], axis=0).T)

    panel[...] = panels[0].T
    weights[0], weights[1] = split(mul3(split(panels[1].T), ordered(first_factor)))
    factor[0], factor[1] = ordered(second_factor)


def natural(part):
    return jnp.concatenate([part[t * 128 : (t + 1) * 128, :] for t in range(8)], axis=1)


def cross_of(part):
    return jnp.concatenate([part[1024:1088, :], part[1088:, :]], axis=1)


def middle_kernel(block, panel, weights, own, got, out, rest):
    cross = split(jnp.concatenate([cross_of(own), cross_of(got)], axis=0))
    rest[...] = panel[...] - mul3((weights[0, :, :128], weights[1, :, :128]), cross)
    proj = split(jnp.concatenate([natural(own)[64:], natural(got)[64:]], axis=0))
    for t in range(2):
        rows = slice(t * 256, (t + 1) * 256)
        out[rows] = block[rows] - mul3((weights[0, rows, :128], weights[1, rows, :128]), proj)


def update_kernel(middle, rest_ref, weights, factor, own, got3, got2, got1, out_ref, out, sems):
    parts = (own, got3, got2, got1)
    cross = split(jnp.concatenate([cross_of(got2), cross_of(got1)], axis=0))
    rest = rest_ref[...] - mul3((weights[0, :, 128:], weights[1, :, 128:]), cross)
    second = split(mul3(split(rest), (factor[0], factor[1])))
    quarters = [natural(part) for part in parts]
    left = [jnp.concatenate([second[i], weights[i, :, 128:]], axis=1) for i in range(2)]
    rows = [quarter[:64] for quarter in quarters] + [quarter[64:] for quarter in quarters[2:]]
    right = split(jnp.concatenate(rows, axis=0))
    stores = []
    for t in range(4):
        at = slice(t * 128, (t + 1) * 128)
        out[at] = middle[at] - mul3((left[0][at], left[1][at]), right)
        stores.append(pltpu.make_async_copy(out.at[at], out_ref.at[at], sems.at[t]))
        stores[t].start()
    for store in stores:
        store.wait()


def call(kernel, outs, args, scratch=(), scalars=0, inputs=None, out_spec=VMEM):
    single = not isinstance(outs, list)
    return pl.pallas_call(
        kernel,
        out_shape=outs,
        in_specs=inputs or [SMEM] * scalars + [VMEM] * (len(args) - scalars),
        out_specs=out_spec if single else [out_spec] * len(outs),
        scratch_shapes=list(scratch),
        compiler_params=PARAMS,
    )(*args)


def shape(*dims, dtype=F32):
    return jax.ShapeDtypeStruct(dims, dtype)


def trade(pieces):
    return lax.all_to_all(pieces, ROW + COL, 0, 0, axis_index_groups=FAR)


def fetch(value, d):
    def partner(i, n, core):
        return (i + 1) % n if i % 2 == core else (i - 1) % n

    pairs = [
        (device(x, y, z, c), device(partner(x, NX, c) if d & 2 else x, partner(y, NY, c) if d & 1 else y, z, c))
        for x in range(NX)
        for y in range(NY)
        for z in range(NZ)
        for c in range(2)
    ]
    return lax.ppermute(value, ROW + COL, pairs)


def local(vectors, reflectors_first, reflectors_second, factor_first, factor_second):
    core = lax.axis_index("core")
    scalar = core.astype(jnp.int32).reshape(1)
    j = label_x(lax.axis_index("x"), core) * 2 + label_y(lax.axis_index("y"), core)
    j = j.astype(jnp.int32).reshape(1)
    shards = jnp.concatenate([reflectors_second, reflectors_first], axis=0)
    mine = lax.all_to_all(jnp.broadcast_to(shards[None], (NZ,) + shards.shape), "z", 0, 0)
    other = lax.ppermute(mine, "core", [(0, 1), (1, 0)])
    block = call(split_kernel, [shape(512, 1024, dtype=BF16)] * 2, (vectors,))
    wide = shape(512, 512, dtype=BF16)
    diagonal, along_x, along_y, *panels = call(
        project_kernel,
        [shape(1152, 128)] * 3 + [shape(256, 256), wide, wide],
        (scalar, j, mine, other, *block),
        (pltpu.VMEM((2, 8, 32, 512), F32),),
        scalars=2,
    )
    half = call(own_kernel, shape(1152, 128), (j, fetch(diagonal, 3), *panels, *block), scalars=1)
    parts = call(near_kernel, shape(8, 144, 128), (half, fetch(along_y, 1), fetch(along_x, 2)))
    parts = call(far_kernel, shape(8, 144, 128), (trade(parts),))
    share = call(share_kernel, shape(1152, 128), (trade(parts),))
    got = {d: fetch(share, d) for d in (3, 2, 1)}
    panel, weights, factor = call(
        prepare_kernel,
        [shape(512, 256), shape(2, 512, 256, dtype=BF16), shape(2, 256, 256, dtype=BF16)],
        (scalar, j, mine, other, factor_second, factor_first),
        (pltpu.VMEM((256, 256), F32), pltpu.VMEM((2, 8, 32, 512), F32), pltpu.VMEM((2, 256, 512), F32)),
        scalars=2,
    )
    middle, rest = call(
        middle_kernel, [shape(512, 1024), shape(512, 256)], (vectors, panel, weights, share, got[3])
    )
    return call(
        update_kernel,
        shape(512, 1024),
        (middle, rest, weights, factor, share, got[3], got[2], got[1]),
        (pltpu.VMEM((512, 1024), F32), pltpu.SemaphoreType.DMA((4,))),
        out_spec=HBM,
    )


def solution(mesh):
    fine = Mesh(mesh.devices.reshape(NX, NY, NZ, 2), ROW + COL)
    return jax.shard_map(
        local,
        mesh=fine,
        in_specs=(P(ROW, COL), P(COL, ROW), P(COL, ROW), P(), P()),
        out_specs=P(ROW, COL),
        check_vma=False,
    )
```

```python
import jax
import jax.numpy as jnp
from jax import lax
from jax.experimental import pallas as pl
from jax.experimental.pallas import tpu as pltpu
from jax.sharding import Mesh, PartitionSpec as P

ROW = ("x", "y")
COL = ("z", "core")
NX, NY, NZ = 4, 8, 8
F32, BF16 = jnp.float32, jnp.bfloat16
VMEM = pl.BlockSpec(memory_space=pltpu.VMEM)
SMEM = pl.BlockSpec(memory_space=pltpu.SMEM)
HBM = pl.BlockSpec(memory_space=pltpu.HBM)
PARAMS = pltpu.CompilerParams(vmem_limit_bytes=48 * 2**20)


def device(x, y, z, core):
    return ((x % NX * NY + y % NY) * NZ + z) * 2 + core


def label_x(x, core):
    return (x >> 1) ^ (x & 1 & ~core)


def label_y(y, core):
    y = (y - core) & 7
    return (y & 1) ^ (y >> 2)


FAR = [
    [
        device(x, y, z, core)
        for x in range(NX)
        for y in range(NY)
        if (label_x(x, core), label_y(y, core)) == (px, py)
    ]
    for z in range(NZ)
    for core in range(2)
    for px in range(2)
    for py in range(2)
]


def split(value):
    high = value.astype(BF16)
    return high, (value - high.astype(F32)).astype(BF16)


def mul(a, b):
    return jnp.dot(a, b, preferred_element_type=F32)


def mul_nt(a, b):
    return lax.dot_general(a, b, (((1,), (1,)), ((), ())), preferred_element_type=F32)


def mul3(a, b, mul=mul):
    return mul(a[0], b[0]) + (mul(a[0], b[1]) + mul(a[1], b[0]))


def split_kernel(block_ref, high, low):
    high[...], low[...] = split(block_ref[...])


def quarter(j, d, high, low, cross, block_high, block_low, out):
    at = pl.ds(pl.multiple_of((j ^ d) * 128, 128), 128)
    rows = high[at, :], low[at, :]
    for t in range(4):
        at = slice(t * 256, (t + 1) * 256)
        value = mul3(rows, (block_high[:, at], block_low[:, at]))
        for half in range(2):
            to = (2 * t + half) * 128
            out[to : to + 128, :] = value[:, half * 128 : (half + 1) * 128]
    at = pl.ds(pl.multiple_of((j ^ d) * 64, 64), 64)
    out[1024:1088, :] = cross[at, :128]
    out[1088:, :] = cross[at, 128:]


def diagonal_kernel(core_ref, j_ref, mine_ref, other_ref, block_high, block_low, out, cross, high, low, both):
    core = core_ref[0]
    both[0] = mine_ref[...]
    both[1] = other_ref[...]
    for c in range(2):
        from_core = both.at[core ^ c]
        for z in range(8):
            for panel in range(2):
                h, l = split(from_core[z, panel * 16 : panel * 16 + 16, :])
                at = (z // 2) * 128 + panel * 64 + (z % 2) * 32 + c * 16
                high[at : at + 16, :] = h
                low[at : at + 16, :] = l

    def whole(panel, ref):
        return jnp.concatenate([ref[q * 128 + panel * 64 : q * 128 + panel * 64 + 64, :] for q in range(4)], axis=0)

    cross[...] = mul3((whole(1, high), whole(1, low)), (whole(0, high), whole(0, low)), mul_nt)
    quarter(j_ref[0], 3, high, low, cross, block_high, block_low, out)


def beside_kernel(j_ref, cross, high, low, block_high, block_low, *outs):
    for d, out in zip((2, 1), outs):
        quarter(j_ref[0], d, high, low, cross, block_high, block_low, out)


def own_kernel(j_ref, got, cross, high, low, block_high, block_low, out):
    quarter(j_ref[0], 0, high, low, cross, block_high, block_low, out)
    out[...] += got[...]


def near_kernel(half, got1, got2, out):
    total = half[...] + (got1[...] + got2[...])
    for m in range(8):
        out[m, :128, :] = total[m * 128 : (m + 1) * 128]
        out[m, 128:, :] = total[1024 + m * 16 : 1040 + m * 16]


def far_kernel(parts, out):
    total = ((parts[0] + parts[1]) + (parts[2] + parts[3])) + ((parts[4] + parts[5]) + (parts[6] + parts[7]))
    for m in range(8):
        out[m] = total


def share_kernel(parts, out):
    for m in range(8):
        out[m * 128 : (m + 1) * 128, :] = parts[m, :128]
        out[1024 + m * 16 : 1040 + m * 16, :] = parts[m, 128:]


ORDER = (0, 3, 2, 1)


def prepare_kernel(
    core_ref, j_ref, mine_ref, other_ref, second_factor, first_factor, panel, weights, factor, turned, both, panels
):
    both[0] = mine_ref[...]
    both[1] = other_ref[...]
    for c in range(2):
        from_core = both.at[core_ref[0] ^ c]
        for z in range(8):
            to = slice(z * 32 + c * 16, z * 32 + c * 16 + 16)
            panels[0, to, :] = from_core[z, :16, :]
            panels[1, to, :] = from_core[z, 16:, :]
    at = [pl.ds(pl.multiple_of((j_ref[0] ^ d) * 64, 64), 64) for d in ORDER]

    def ordered(ref):
        turned[...] = ref[...].T
        return split(jnp.concatenate([turned[rows, :] for rows in at], axis=0).T)

    panel[...] = panels[0].T
    weights[0], weights[1] = split(mul3(split(panels[1].T), ordered(first_factor)))
    factor[0], factor[1] = ordered(second_factor)


def natural(part):
    return jnp.concatenate([part[t * 128 : (t + 1) * 128, :] for t in range(8)], axis=1)


def cross_of(part):
    return jnp.concatenate([part[1024:1088, :], part[1088:, :]], axis=1)


def middle_kernel(block, panel, weights, own, got, out, rest):
    cross = split(jnp.concatenate([cross_of(own), cross_of(got)], axis=0))
    rest[...] = panel[...] - mul3((weights[0, :, :128], weights[1, :, :128]), cross)
    proj = split(jnp.concatenate([natural(own)[64:], natural(got)[64:]], axis=0))
    for t in range(2):
        rows = slice(t * 256, (t + 1) * 256)
        out[rows] = block[rows] - mul3((weights[0, rows, :128], weights[1, rows, :128]), proj)


def update_kernel(middle, rest_ref, weights, factor, own, got3, got2, got1, out_ref, out, sems):
    parts = (own, got3, got2, got1)
    cross = split(jnp.concatenate([cross_of(got2), cross_of(got1)], axis=0))
    rest = rest_ref[...] - mul3((weights[0, :, 128:], weights[1, :, 128:]), cross)
    second = split(mul3(split(rest), (factor[0], factor[1])))
    quarters = [natural(part) for part in parts]
    left = [jnp.concatenate([second[i], weights[i, :, 128:]], axis=1) for i in range(2)]
    rows = [quarter[:64] for quarter in quarters] + [quarter[64:] for quarter in quarters[2:]]
    right = split(jnp.concatenate(rows, axis=0))
    stores = []
    for t in range(2):
        at = slice(t * 256, (t + 1) * 256)
        tile = left[0][at], left[1][at]
        for half in range(2):
            columns = slice(half * 512, (half + 1) * 512)
            out[at, columns] = middle[at, columns] - mul3(tile, (right[0][:, columns], right[1][:, columns]))
        stores.append(pltpu.make_async_copy(out.at[at], out_ref.at[at], sems.at[t]))
        stores[t].start()
    for store in stores:
        store.wait()


def call(kernel, outs, args, scratch=(), scalars=0, inputs=None, out_spec=VMEM):
    single = not isinstance(outs, list)
    return pl.pallas_call(
        kernel,
        out_shape=outs,
        in_specs=inputs or [SMEM] * scalars + [VMEM] * (len(args) - scalars),
        out_specs=out_spec if single else [out_spec] * len(outs),
        scratch_shapes=list(scratch),
        compiler_params=PARAMS,
    )(*args)


def shape(*dims, dtype=F32):
    return jax.ShapeDtypeStruct(dims, dtype)


def trade(pieces):
    return lax.all_to_all(pieces, ROW + COL, 0, 0, axis_index_groups=FAR)


def fetch(value, d):
    def partner(i, n, core):
        return (i + 1) % n if i % 2 == core else (i - 1) % n

    pairs = [
        (device(x, y, z, c), device(partner(x, NX, c) if d & 2 else x, partner(y, NY, c) if d & 1 else y, z, c))
        for x in range(NX)
        for y in range(NY)
        for z in range(NZ)
        for c in range(2)
    ]
    return lax.ppermute(value, ROW + COL, pairs)


def local(vectors, reflectors_first, reflectors_second, factor_first, factor_second):
    core = lax.axis_index("core")
    scalar = core.astype(jnp.int32).reshape(1)
    j = label_x(lax.axis_index("x"), core) * 2 + label_y(lax.axis_index("y"), core)
    j = j.astype(jnp.int32).reshape(1)
    shards = jnp.concatenate([reflectors_second, reflectors_first], axis=0)
    mine = lax.all_to_all(jnp.broadcast_to(shards[None], (NZ,) + shards.shape), "z", 0, 0)
    other = lax.ppermute(mine, "core", [(0, 1), (1, 0)])
    block = call(split_kernel, [shape(512, 1024, dtype=BF16)] * 2, (vectors,))
    wide = shape(512, 512, dtype=BF16)
    diagonal, *panels = call(
        diagonal_kernel,
        [shape(1152, 128), shape(256, 256), wide, wide],
        (scalar, j, mine, other, *block),
        (pltpu.VMEM((2, 8, 32, 512), F32),),
        scalars=2,
    )
    along_x, along_y = call(beside_kernel, [shape(1152, 128)] * 2, (j, *panels, *block), scalars=1)
    half = call(own_kernel, shape(1152, 128), (j, fetch(diagonal, 3), *panels, *block), scalars=1)
    parts = call(near_kernel, shape(8, 144, 128), (half, fetch(along_y, 1), fetch(along_x, 2)))
    parts = call(far_kernel, shape(8, 144, 128), (trade(parts),))
    share = call(share_kernel, shape(1152, 128), (trade(parts),))
    got = {d: fetch(share, d) for d in (3, 2, 1)}
    panel, weights, factor = call(
        prepare_kernel,
        [shape(512, 256), shape(2, 512, 256, dtype=BF16), shape(2, 256, 256, dtype=BF16)],
        (scalar, j, mine, other, factor_second, factor_first),
        (pltpu.VMEM((256, 256), F32), pltpu.VMEM((2, 8, 32, 512), F32), pltpu.VMEM((2, 256, 512), F32)),
        scalars=2,
    )
    middle, rest = call(
        middle_kernel, [shape(512, 1024), shape(512, 256)], (vectors, panel, weights, share, got[3])
    )
    return call(
        update_kernel,
        shape(512, 1024),
        (middle, rest, weights, factor, share, got[3], got[2], got[1]),
        (pltpu.VMEM((512, 1024), F32), pltpu.SemaphoreType.DMA((2,))),
        out_spec=HBM,
    )


def solution(mesh):
    fine = Mesh(mesh.devices.reshape(NX, NY, NZ, 2), ROW + COL)
    return jax.shard_map(
        local,
        mesh=fine,
        in_specs=(P(ROW, COL), P(COL, ROW), P(COL, ROW), P(), P()),
        out_specs=P(ROW, COL),
        check_vma=False,
    )
```
